768 devices in a mesh: dp: 64 (over x, y, core), text: 12 (over z).
Axes of the slice: x: 4, y: 8, z: 12, core: 2. Of those that a mesh axis runs over, the one named last changes fastest.
Arguments:
- regions: bfloat16 [128, 900, 256], P('dp', 'text'), may hold values from -6 to 6
- words: bfloat16 [128, 144, 256], P('dp', 'text'), may hold values from -6 to 6
- box_counts: int32 [128], P('dp'), may hold values from 100 to 900, as said below
- token_counts: int32 [128], P('dp'), may hold values from 72 to 144, as said below
- span_begin: int32 [128, 900], P('dp', 'text'), may hold values from 0 to 68
- span_length: int32 [128, 900], P('dp', 'text'), may hold values from 1 to 4
- bias_weight: float32 [256], replicated, may hold values from -0.375 to 0.375
- logit_bias: float32 [], replicated, may hold values from -1 to 0.5
- loss_scale: float32 [], replicated, may hold values from 512 to 2048
Outputs:
- region_grad: bfloat16 [128, 900, 256], P('dp', 'text')
- word_grad: bfloat16 [128, 144, 256], P('dp', 'text')
The draws below stay inside these ranges and needn't reach their ends.
Inputs may be any that keep to these rules, and one draw needn't show every extreme that they name: `box_counts`: some image has exactly 900 boxes and some exactly 100. `token_counts`: some caption has exactly 144 tokens and some exactly 72.
All inputs are finite; a program needn't handle non-finite values.
Results may differ from the reference program's by a relative error of at most 0.0034.
Values may be sent and summed in bfloat16 or wider, within the bound.
A program may use at most 64 MiB of HBM per device.

```python
import math
import jax
import jax.numpy as jnp
from jax import lax

D = 256
IMAGES = 128
BOXES = 900
TOKENS_CAP = 144


def bounded_counts(key, total, lowest, highest):
    first_key, second_key, third_key = jax.random.split(key, 3)
    counts = jax.random.randint(first_key, (total,), lowest, highest + 1, dtype=jnp.int32)
    first = jax.random.randint(second_key, (), 0, total, dtype=jnp.int32)
    second = (first + 1 + jax.random.randint(third_key, (), 0, total - 1, dtype=jnp.int32)) % total
    return counts.at[first].set(highest).at[second].set(lowest)


def draw_box_counts(key, part):
    key = jax.random.fold_in(key, 11)
    return bounded_counts(key, IMAGES, BOXES // 9, BOXES)


def draw_token_counts(key, part):
    key = jax.random.fold_in(key, 13)
    return bounded_counts(key, IMAGES, TOKENS_CAP // 2, TOKENS_CAP)


def place_ends(entries, key, low, top_value):
    longest = entries.shape.index(max(entries.shape))
    spots = []
    for shift in (0, 1):
        where = [jax.random.randint(jax.random.fold_in(key, axis), (), 0, length) for axis, length in enumerate(entries.shape)]
        where[longest] = (where[longest] + shift) % entries.shape[longest]
        spots.append(tuple(where))
    return entries.at[spots[0]].set(low).at[spots[1]].set(top_value)


def steps_of(key, extent, shards, least, top_value):
    def one(position, parts):
        draws = jax.random.uniform(jax.random.fold_in(jax.random.fold_in(key, 6), position), (parts,), jnp.float32, least / len(shards), top_value / len(shards))
        return jnp.repeat(jnp.exp(draws), extent[position] // parts).reshape((-1,) + (1,) * (len(extent) - position - 1))

    level = one(*shards[0])
    for cut in shards[1:]:
        level = level * one(*cut)
    return level


def normal_values(stream_key, extent, scale, reach, pieces=(), held_as=jnp.bfloat16):
    result = scale * jax.random.normal(stream_key, extent, jnp.float32)
    if pieces:
        result = result * steps_of(stream_key, extent, pieces, -0.22, 0.18)
    return jnp.clip(result, -reach, reach).astype(held_as)


def setup_inputs(seed: int = 0) -> dict:
    splits = jax.random.split(jax.random.key(seed), 10)
    regions = normal_values(splits[0], (IMAGES, BOXES, D), 1.0, 6.0, ((0, 64), (1, 12)))
    words = normal_values(splits[1], (IMAGES, TOKENS_CAP, D), 1.0, 6.0, ((0, 64), (1, 12)))
    box_counts = draw_box_counts(jax.random.fold_in(splits[9], 71), 0)
    token_counts = draw_token_counts(jax.random.fold_in(splits[9], 71), 0)
    span_begin = place_ends(jax.random.randint(splits[4], (IMAGES, BOXES), 0, TOKENS_CAP // 2 - 3), jax.random.fold_in(splits[4], 1), 0, (TOKENS_CAP // 2 - 3) - 1).astype(jnp.int32)
    span_length = place_ends(jax.random.randint(splits[5], (IMAGES, BOXES), 1, 5), jax.random.fold_in(splits[5], 1), 1, 4).astype(jnp.int32)
    bias_weight = normal_values(splits[6], (D,), D ** -0.5, 0.375, (), jnp.float32)
    logit_bias = jnp.clip(jax.random.uniform(splits[7], (), jnp.float32, -1.0, 0.5), -1.0, 0.5)
    loss_scale = jnp.clip(jnp.exp(jax.random.uniform(splits[8], (), jnp.float32, math.log(512.0), math.log(2048.0))), 512.0, 2048.0)
    return {"regions": regions, "words": words, "box_counts": box_counts, "token_counts": token_counts, "span_begin": span_begin, "span_length": span_length, "bias_weight": bias_weight, "logit_bias": logit_bias, "loss_scale": loss_scale}


focal_alpha = 0.25

def focal_slope(score, positive):
    prob = jax.nn.sigmoid(score)
    log_prob = -jax.nn.softplus(-score)
    log_rest = -jax.nn.softplus(score)
    rest = 1.0 - prob
    pos_slope = focal_alpha * rest * rest * (2.0 * prob * log_prob - rest)
    neg_slope = (1.0 - focal_alpha) * prob * prob * (prob - 2.0 * rest * log_rest)
    return jnp.where(positive, pos_slope, neg_slope)

def reference(regions, words, box_counts, token_counts, span_begin, span_length, bias_weight, logit_bias, loss_scale):
    n_images, n_boxes, width = regions.shape
    n_tokens = words.shape[1]
    box_index = jnp.arange(n_boxes, dtype=jnp.int32)
    box_valid = box_index[None, :] < box_counts[:, None]
    positives = jnp.sum(jnp.where(box_valid, span_length, 0)).astype(jnp.float32)
    coef = loss_scale / positives
    inverse_root = 1.0 / jnp.sqrt(jnp.float32(width))
    flattened = regions.reshape(n_images * n_boxes, width)
    valid_rows = box_valid.reshape(-1)
    row_image = jnp.repeat(jnp.arange(n_images, dtype=jnp.int32), n_boxes)
    begin_rows = span_begin.reshape(-1)
    end_rows = begin_rows + span_length.reshape(-1)
    token_index = jnp.arange(n_tokens, dtype=jnp.int32)

    def one_caption(totals, inputs):
        caption, tok_count, caption_index = inputs
        bias_row = jnp.dot(caption.astype(jnp.float32), bias_weight, precision=lax.Precision.HIGHEST) + logit_bias
        scores = jnp.dot(flattened, caption.T, preferred_element_type=jnp.float32) * inverse_root + bias_row[None, :]
        positive = (row_image == caption_index)[:, None] & (token_index[None, :] >= begin_rows[:, None]) & (token_index[None, :] < end_rows[:, None])
        valid = valid_rows[:, None] & (token_index < tok_count)[None, :]
        slope = jnp.where(valid, focal_slope(scores, positive), jnp.float32(0.0))
        slope_half = slope.astype(jnp.bfloat16)
        totals = totals + jnp.dot(slope_half, caption, preferred_element_type=jnp.float32) * inverse_root
        word_part = jnp.dot(slope_half.T, flattened, preferred_element_type=jnp.float32) * inverse_root
        word_part = word_part + lax.optimization_barrier(jnp.sum(slope, axis=0))[:, None] * bias_weight[None, :]
        return (totals, word_part)
    start_totals = jnp.zeros((n_images * n_boxes, width), jnp.float32)
    region_sum, word_sum = lax.scan(one_caption, start_totals, (words, token_counts, jnp.arange(n_images, dtype=jnp.int32)))
    region_grad = (region_sum * coef).reshape(n_images, n_boxes, width).astype(jnp.bfloat16)
    word_grad = (word_sum * coef).astype(jnp.bfloat16)
    return (region_grad, word_grad)
```

```python
import functools
import math

import jax
import jax.numpy as jnp
from jax import lax
from jax.experimental import pallas as pl
from jax.experimental.pallas import tpu as pltpu
from jax.sharding import PartitionSpec as P

MESH = pl.DeviceIdType.MESH
NX, NY, NZ = 4, 8, 12
D = 256
HALF = 128
BOX = 75
BOXP = 80
RB = 2 * BOXP
TOK = 12
CB = 48
XB = NZ * CB
ROWS = NY * RB
TOKS = NX * XB
FEAT = D + 16
BF = jnp.bfloat16
F32 = jnp.float32
LOG2E = math.log2(math.e)


def place():
    dp = lax.axis_index("dp")
    return dp // (NY * 2), (dp // 2) % NY, dp % 2, lax.axis_index("text")


def device(x, y, c, z):
    return ((x % NX) * NY + (y % NY)) * 2 + c, z % NZ


def copy_to(src, dst, sems, k, dev):
    send, recv = sems
    return pltpu.make_async_remote_copy(
        src_ref=src,
        dst_ref=dst,
        send_sem=send.at[k],
        recv_sem=recv.at[k],
        device_id=dev,
        device_id_type=MESH,
    )


def enter(peers):
    barrier = pltpu.get_barrier_semaphore()
    for dev in peers:
        pl.semaphore_signal(barrier, inc=1, device_id=dev, device_id_type=MESH)
    pl.semaphore_wait(barrier, len(peers))


def iota(shape, dim):
    return lax.broadcasted_iota(jnp.int32, shape, dim)


def prepare(regions, words, spans, box_counts, token_counts, rows, own, wide, z):
    count = jnp.zeros((1, 1), F32)
    for img in range(2):
        valid = BOX * z + iota((1, BOX), 1) < box_counts[img]
        length = jnp.where(valid, spans[img : img + 1, :], 0).astype(F32)
        count = count + jnp.sum(length, axis=1, keepdims=True)
    high = jnp.floor(count * (1.0 / 16.0))
    low = count - 16.0 * high
    lane = iota((BOXP, D), 1)
    row = iota((BOXP, D), 0)
    slot = jnp.where(lane < BOXP, lane, lane - BOXP)
    limit = jnp.where(lane < BOXP, box_counts[0], box_counts[1])
    flag = (slot < BOX) & (lane < RB) & (BOX * z + slot < limit)
    wide[...] = jnp.zeros_like(wide)
    for img in range(2):
        wide[img * BOXP : img * BOXP + BOX, :] = regions[img].astype(F32)
    for img in range(2):
        value = wide[img * BOXP : (img + 1) * BOXP, :]
        value = jnp.where(BOX * z + row < box_counts[img], value, 0.0)
        value = jnp.where(row < BOX, value, 0.0)
        if img == 0:
            value = jnp.where((row == BOX) & flag, 1.0, value)
            value = jnp.where((row == BOX + 1) & (lane == 0), high, value)
            value = jnp.where((row == BOX + 1) & (lane == 1), low, value)
        rows[0, img * BOXP : (img + 1) * BOXP, :] = value.astype(BF)
    own[...] = jnp.zeros_like(own)
    tok = iota((TOK, D), 0)
    for cap in range(2):
        value = words[cap].astype(F32)
        value = jnp.where(TOK * z + tok < token_counts[cap], value, 0.0)
        own[cap * TOK : (cap + 1) * TOK, :] = value


def gather_kernel(
    box_counts, token_counts, regions, words, spans, rows, toks,
    wide, own, pair, sent, got, y_send, y_recv, z_send, z_recv, x_send, x_recv, c_send, c_recv,
):
    x, y, c, z = place()
    ysem, zsem, xsem, csem = (y_send, y_recv), (z_send, z_recv), (x_send, x_recv), (c_send, c_recv)
    twin = device(x, y, 1 - c, z)
    up, down = device(x, y + 1, c, z), device(x, y + NY - 1, c, z)
    east, west = device(x + 1, y, c, z), device(x + NX - 1, y, c, z)
    prepare(regions, words, spans, box_counts, token_counts, rows, own, wide, z)
    sent[...] = own[...].astype(BF)
    enter([twin, up, down, east, west] + [device(x, y, c, z + k) for k in range(1, NZ)])

    swap = copy_to(sent, got, csem, 0, twin)
    swap.start()

    def y_up(step):
        slot = (NY + 1 - step) % NY
        part = pl.ds(0, RB if step < 4 else BOXP)
        return copy_to(rows.at[slot, part], rows.at[NY - step, part], ysem, step - 1, up)

    def y_down(step):
        part = pl.ds(0, RB) if step < 4 else pl.ds(BOXP, BOXP)
        return copy_to(rows.at[step - 1, part], rows.at[step, part], ysem, 3 + step, down)

    y_up(1).start()
    y_down(1).start()

    swap.wait()
    mine = own[0:24, :]
    other = got[0:24, :].astype(F32)
    pair[0:24, :] = jnp.where(c == 0, mine, other)
    pair[24:48, :] = jnp.where(c == 0, other, mine)
    toks[c, 0:CB, :] = jnp.where(c == 0, pair[:, 0:HALF], pair[:, HALF:D]).astype(BF)

    def z_copy(k):
        return copy_to(
            toks.at[c, pl.ds(0, CB)], toks.at[c, pl.ds((NZ - k) * CB, CB)], zsem, k - 1, device(x, y, c, z + k)
        )

    order = [1, 11, 2, 10, 3, 9, 4, 8, 5, 7, 6]
    for k in order:
        z_copy(k).start()

    def y_step(step):
        y_up(step - 1).wait_recv()
        y_up(step).start()
        y_down(step - 1).wait_recv()
        y_down(step).start()

    y_step(2)
    for k in order:
        z_copy(k).wait_recv()

    whole, first, second = pl.ds(0, XB), pl.ds(2 * XB, XB // 2), pl.ds(2 * XB + XB // 2, XB // 2)
    at_three, at_one = pl.ds(3 * XB, XB), pl.ds(XB, XB)
    go_east = copy_to(toks.at[c, whole], toks.at[c, at_three], xsem, 0, east)
    go_west = copy_to(toks.at[c, whole], toks.at[c, at_one], xsem, 1, west)
    more_east = copy_to(toks.at[c, pl.ds(3 * XB, XB // 2)], toks.at[c, first], xsem, 2, east)
    more_west = copy_to(toks.at[c, pl.ds(XB + XB // 2, XB // 2)], toks.at[c, second], xsem, 3, west)

    def to_twin(part, k):
        return copy_to(toks.at[c, part], toks.at[c, part], csem, 1 + k, twin)

    twins = [to_twin(part, k) for k, part in enumerate((whole, at_three, at_one, first, second))]

    def from_twin(part, k):
        return copy_to(toks.at[1 - c, part], toks.at[1 - c, part], csem, 1 + k, twin)

    arrivals = [from_twin(part, k) for k, part in enumerate((whole, at_three, at_one, first, second))]
    go_east.start()
    go_west.start()
    twins[0].start()
    y_step(3)
    go_east.wait_recv()
    more_east.start()
    twins[1].start()
    go_west.wait_recv()
    more_west.start()
    twins[2].start()
    y_step(4)
    more_east.wait_recv()
    twins[3].start()
    more_west.wait_recv()
    twins[4].start()
    y_up(4).wait_recv()
    y_down(4).wait_recv()
    for arrival in arrivals:
        arrival.wait_recv()
    for step in range(1, 5):
        y_up(step).wait_send()
        y_down(step).wait_send()
    for k in range(1, NZ):
        z_copy(k).wait_send()
    for copy in [go_east, go_west, more_east, more_west] + twins:
        copy.wait_send()


def gather(regions, words, box_counts, token_counts, span_length):
    vmem, smem = pl.BlockSpec(memory_space=pltpu.VMEM), pl.BlockSpec(memory_space=pltpu.SMEM)
    sems = lambda n: [pltpu.SemaphoreType.DMA((n,))] * 2
    return pl.pallas_call(
        gather_kernel,
        out_shape=(
            jax.ShapeDtypeStruct((NY, RB, D), BF),
            jax.ShapeDtypeStruct((2, TOKS, HALF), BF),
        ),
        in_specs=[smem, smem, vmem, vmem, vmem],
        out_specs=(vmem, vmem),
        scratch_shapes=[
            pltpu.VMEM((RB, D), F32),
            pltpu.VMEM((32, D), F32),
            pltpu.VMEM((CB, D), F32),
            pltpu.VMEM((32, D), BF),
            pltpu.VMEM((32, D), BF),
        ]
        + sems(8) + sems(NZ - 1) + sems(4) + sems(6),
        compiler_params=pltpu.CompilerParams(
            collective_id=0, has_side_effects=True, vmem_limit_bytes=40 * 2**20
        ),
        name="gather",
    )(box_counts, token_counts, regions, words, span_length)


def negative_slope(score):
    grown = jnp.exp2(jnp.minimum(score, 100.0))
    total = 1.0 + grown
    rest = 1.0 / total
    prob = grown * rest
    lost = jnp.log(total) + (grown - (total - 1.0))
    return prob * prob * (0.5 * prob + rest * lost)


def positive_slope(score):
    small = jnp.exp2(-jnp.abs(score))
    part = 1.0 / (1.0 + small)
    prob = jnp.where(score >= 0.0, part, small * part)
    rest = jnp.where(score >= 0.0, small * part, part)
    lost = jnp.log(1.0 + small) + (small - ((1.0 + small) - 1.0)) + jnp.maximum(-score, 0.0) * math.log(2.0)
    return (-1.0 / 6.0) * rest * rest * (2.0 * prob * lost + rest)


def word_scores_bias(pieces, words_t, logit):
    rows = jnp.dot(pieces, words_t, preferred_element_type=F32)
    return (rows[0:1] + rows[1:2] + rows[2:3] + logit) * LOG2E


def split_bias(bias):
    first = bias.astype(BF)
    left = bias - first.astype(F32)
    second = left.astype(BF)
    third = (left - second.astype(F32)).astype(BF)
    row = iota((16, D), 0)
    value = jnp.where(row == 0, first.astype(F32), 0.0)
    value = jnp.where(row == 1, second.astype(F32), value)
    value = jnp.where(row == 2, third.astype(F32), value)
    return value.astype(BF)


def to_column(row, n):
    return jnp.transpose(jnp.broadcast_to(row, (128, n)))[:, 0:1]


TB = 256
CHUNK = 256


def compute_kernel(
    logit, rows, toks, bias, begin, length, region_out, word_out, count_out, flat, flat_t, total
):
    dp = lax.axis_index("dp")
    z = lax.axis_index("text")
    lane = iota((RB, D), 1)
    row = iota((RB, D), 0)
    counts = jnp.zeros((1, 1), F32)
    pad = (row % BOXP) >= BOX
    for slot in range(NY):
        value = rows[slot].astype(F32)
        info = value[BOX + 1 : BOX + 2, :]
        counts = counts + 16.0 * info[:, 0:1] + info[:, 1:2]
        flags = jnp.broadcast_to(value[BOX : BOX + 1, 0:RB], (16, RB))
        clean = jnp.where(pad, 0.0, value)
        flat[slot * RB : (slot + 1) * RB, :] = clean.astype(BF)
        flat_t[0:D, slot * RB : (slot + 1) * RB] = jnp.transpose(clean).astype(BF)
        first = iota((16, RB), 0) == 0
        flat_t[D:FEAT, slot * RB : (slot + 1) * RB] = jnp.where(first, flags, 0.0).astype(BF)
    count_out[...] = jnp.broadcast_to(counts, (8, 128))
    bias_row = bias[...]
    pieces = split_bias(bias_row)
    bias_column = to_column(bias_row, D) * 16.0
    logit_value = logit[0]

    total[...] = jnp.zeros_like(total)

    def one_tile(t, _):
        part = pl.ds(pl.multiple_of(t * TB, TB), TB)
        words = jnp.concatenate([toks[0, part, :], toks[1, part, :]], axis=1)
        words_t = jnp.transpose(words)
        offset = word_scores_bias(pieces, words_t, logit_value)
        grads = jnp.zeros((FEAT, TB), F32)
        for r in range(ROWS // CHUNK):
            span = slice(r * CHUNK, (r + 1) * CHUNK)
            score = jnp.dot(flat[span, :], words_t, preferred_element_type=F32)
            slope = negative_slope(score * (LOG2E / 16.0) + offset).astype(BF)
            total[span, :] += jnp.dot(slope, words, preferred_element_type=F32)
            grads = grads + jnp.dot(flat_t[:, span], slope, preferred_element_type=F32)
        full = grads[0:D, :] + bias_column * grads[D : D + 1, :]
        back = jnp.transpose(full)
        word_out[0, part, :] = back[:, 0:HALF]
        word_out[1, part, :] = back[:, HALF:D]
        return 0

    lax.fori_loop(0, TOKS // TB, one_tile, 0)

    words = jnp.concatenate([toks[0, 0:XB, :], toks[1, 0:XB, :]], axis=1)
    words_t = jnp.transpose(words.astype(F32)).astype(BF)
    offset = word_scores_bias(pieces, words_t, logit_value)
    col = iota((1, XB), 1)
    slot = col % CB
    core = dp % 2
    token = ((z + col // CB) % NZ) * TOK + slot % TOK
    caption = jnp.where(slot // (2 * TOK) == core, (slot // TOK) % 2, -1)
    own = flat[0:RB, :]
    score = jnp.dot(own, words_t, preferred_element_type=F32) * (LOG2E / 16.0) + offset
    eye = iota((BOXP, BOXP), 0) == iota((BOXP, BOXP), 1)

    def column(ref, img):
        line = jnp.concatenate([ref[img : img + 1, :], jnp.zeros((1, BOXP - BOX), jnp.int32)], axis=1)
        return jnp.sum(jnp.where(eye, line, 0).astype(F32), axis=1, keepdims=True).astype(jnp.int32)

    deltas = []
    for img in range(2):
        start = column(begin, img)
        stop = start + column(length, img)
        positive = (caption == img) & (token >= start) & (token < stop)
        part = score[img * BOXP : (img + 1) * BOXP, :]
        change = positive_slope(part).astype(BF).astype(F32) - negative_slope(part).astype(BF).astype(F32)
        deltas.append(jnp.where(positive, change, 0.0))
    delta = jnp.concatenate(deltas, axis=0)
    total[0:RB, :] += jnp.dot(delta.astype(BF), words, preferred_element_type=F32)
    flipped = jnp.transpose(delta).astype(BF)
    more = jnp.dot(flipped, own, preferred_element_type=F32)
    flagged = jnp.transpose(flat_t[D:FEAT, 0:RB].astype(F32))
    sums = jnp.dot(flipped, flagged.astype(BF), preferred_element_type=F32)[:, 0:1]
    more = more + sums * (16.0 * bias_row)
    for half in range(2):
        word_out[half, 0:XB, :] += more[:, half * HALF : (half + 1) * HALF]
    for slot_index in range(NY):
        region_out[slot_index] = total[slot_index * RB : (slot_index + 1) * RB, :].astype(region_out.dtype)


def compute(rows, toks, bias_weight, logit_bias, span_begin, span_length):
    vmem, smem = pl.BlockSpec(memory_space=pltpu.VMEM), pl.BlockSpec(memory_space=pltpu.SMEM)
    return pl.pallas_call(
        compute_kernel,
        out_shape=(
            jax.ShapeDtypeStruct((NY, RB, D), F32),
            jax.ShapeDtypeStruct((2, TOKS, HALF), F32),
            jax.ShapeDtypeStruct((8, 128), F32),
        ),
        in_specs=[smem] + [vmem] * 5,
        out_specs=(vmem, vmem, vmem),
        scratch_shapes=[
            pltpu.VMEM((ROWS, D), BF),
            pltpu.VMEM((FEAT, ROWS), BF),
            pltpu.VMEM((ROWS, D), F32),
        ],
        compiler_params=pltpu.CompilerParams(vmem_limit_bytes=48 * 2**20),
        name="pairs",
    )(logit_bias.reshape(1), rows, toks, bias_weight.reshape(1, D), span_begin, span_length)


def scatter_kernel(
    box_counts, token_counts, scale, regions, words, counts, region_out, word_out,
    tally, tally_c, tally_x, tally_z, stage, stage_in, acc, y_out, y_in, x_out, x_in, z_out, z_in, last, last_in,
    y_send, y_recv, z_send, z_recv, x_send, x_recv, c_send, c_recv, n_send, n_recv,
):
    x, y, c, z = place()
    ysem, zsem, xsem, csem = (y_send, y_recv), (z_send, z_recv), (x_send, x_recv), (c_send, c_recv)
    nsem = (n_send, n_recv)
    twin = device(x, y, 1 - c, z)
    up, down = device(x, y + 1, c, z), device(x, y + NY - 1, c, z)
    east, west, far = device(x + 1, y, c, z), device(x + NX - 1, y, c, z), device(x + 2, y, c, z)
    stage[...] = words[1 - c].astype(BF)
    enter([twin, up, down, east, west, far] + [device(x, y, c, z + k) for k in range(1, NZ)])

    swap = copy_to(stage, stage_in, csem, 0, twin)
    swap.start()
    count_c = copy_to(counts, tally_c, nsem, 0, twin)
    count_c.start()

    def y_up(step):
        part = pl.ds(0, BOXP if step == 1 else RB)
        return copy_to(y_out.at[step - 1, part], y_in.at[step - 1, part], ysem, step - 1, up)

    def y_down(step):
        part = pl.ds(BOXP, BOXP) if step == 1 else pl.ds(0, RB)
        return copy_to(y_out.at[3 + step, part], y_in.at[3 + step, part], ysem, 3 + step, down)

    def y_step(step):
        upper, lower = 5 - step, 3 + step
        up_sum, down_sum = regions[upper], regions[lower % NY]
        if step == 1:
            y_out[0, 0:BOXP, :] = up_sum[0:BOXP].astype(BF)
            y_out[4, BOXP:RB, :] = up_sum[BOXP:RB].astype(BF)
        else:
            y_up(step - 1).wait_recv()
            if step == 2:
                y_out[1, 0:BOXP, :] = (up_sum[0:BOXP] + y_in[0, 0:BOXP].astype(F32)).astype(BF)
                y_out[1, BOXP:RB, :] = up_sum[BOXP:RB].astype(BF)
            else:
                y_out[step - 1] = (up_sum + y_in[step - 2].astype(F32)).astype(BF)
        y_up(step).start()
        if step > 1:
            y_down(step - 1).wait_recv()
            if step == 2:
                y_out[5, 0:BOXP, :] = down_sum[0:BOXP].astype(BF)
                y_out[5, BOXP:RB, :] = (down_sum[BOXP:RB] + y_in[4, BOXP:RB].astype(F32)).astype(BF)
            else:
                y_out[3 + step] = (down_sum + y_in[2 + step].astype(F32)).astype(BF)
        y_down(step).start()

    y_step(1)

    swap.wait_recv()
    acc[...] = words[c] + stage_in[...].astype(F32)
    count_c.wait_recv()
    tally[0] = counts[...] + tally_c[...]

    middle = XB // 2
    x_out[0, 0:middle, :] = acc[2 * XB : 2 * XB + middle, :].astype(BF)
    x_out[1, middle:XB, :] = acc[2 * XB + middle : 3 * XB, :].astype(BF)
    near_east = copy_to(x_out.at[0, pl.ds(0, middle)], x_in.at[0, pl.ds(0, middle)], xsem, 0, east)
    near_west = copy_to(x_out.at[1, pl.ds(middle, middle)], x_in.at[1, pl.ds(middle, middle)], xsem, 1, west)
    full_east = copy_to(x_out.at[2], x_in.at[2], xsem, 2, east)
    full_west = copy_to(x_out.at[3], x_in.at[3], xsem, 3, west)
    near_east.start()
    near_west.start()
    counts_x = [copy_to(tally.at[0], tally_x.at[k], nsem, 1 + k, dev) for k, dev in enumerate((east, west, far))]
    for copy in counts_x:
        copy.start()
    y_step(2)
    near_east.wait_recv()
    x_out[2, 0:middle, :] = (acc[XB : XB + middle, :] + x_in[0, 0:middle].astype(F32)).astype(BF)
    x_out[2, middle:XB, :] = acc[XB + middle : 2 * XB, :].astype(BF)
    full_east.start()
    near_west.wait_recv()
    x_out[3, 0:middle, :] = acc[3 * XB : 3 * XB + middle, :].astype(BF)
    x_out[3, middle:XB, :] = (acc[3 * XB + middle : 4 * XB, :] + x_in[1, middle:XB].astype(F32)).astype(BF)
    full_west.start()
    for copy in counts_x:
        copy.wait_recv()
    tally[1] = tally[0] + tally_x[0] + tally_x[1] + tally_x[2]
    y_step(3)
    full_east.wait_recv()
    full_west.wait_recv()
    z_out[...] = acc[0:XB, :] + x_in[2].astype(F32) + x_in[3].astype(F32)
    stage_z = x_in
    stage_z[0] = z_out[...].astype(BF)

    def z_copy(k):
        return copy_to(
            stage_z.at[0, pl.ds(k * CB, CB)], z_in.at[pl.ds((k - 1) * CB, CB)], zsem, k - 1, device(x, y, c, z + k)
        )

    def z_count(k):
        return copy_to(tally.at[1], tally_z.at[k - 1], nsem, 3 + k, device(x, y, c, z + k))

    order = [6, 5, 7, 4, 8, 3, 9, 2, 10, 1, 11]
    for k in order:
        z_copy(k).start()
    for k in order:
        z_count(k).start()
    y_step(4)
    for k in order:
        z_count(k).wait_recv()
    positives = tally[1]
    for k in range(1, NZ):
        positives = positives + tally_z[k - 1]
    coef = (scale[0] * (1.5 / 16.0)) / positives[0:1, 0:1]

    chip = z_out[0:CB, :]
    for k in order:
        z_copy(k).wait_recv()
    for k in range(1, NZ):
        chip = chip + z_in[(k - 1) * CB : k * CB, :].astype(F32)
    keep = jnp.where(c == 0, chip[0:24], chip[24:48])
    last[...] = jnp.where(c == 0, chip[24:48], chip[0:24])
    final = copy_to(last, last_in, csem, 1, twin)
    final.start()

    y_up(4).wait_recv()
    y_down(4).wait_recv()
    row = iota((BOXP, 1), 0)
    for img in range(2):
        span = slice(img * BOXP, (img + 1) * BOXP)
        value = regions[0, span, :] + y_in[3, span].astype(F32) + y_in[7, span].astype(F32)
        value = jnp.where(BOX * z + row < box_counts[img], value * coef, 0.0)
        region_out[img] = value[0:BOX].astype(BF)

    final.wait_recv()
    theirs = last_in[...]
    value = jnp.concatenate([jnp.where(c == 0, keep, theirs), jnp.where(c == 0, theirs, keep)], axis=1)
    tok = iota((24, 1), 0)
    for cap in range(2):
        part = value[cap * TOK : (cap + 1) * TOK] * coef
        word_out[cap] = jnp.where(TOK * z + tok[0:TOK] < token_counts[cap], part, 0.0).astype(BF)

    for step in range(1, 5):
        y_up(step).wait_send()
        y_down(step).wait_send()
    for k in range(1, NZ):
        z_copy(k).wait_send()
        z_count(k).wait_send()
    for copy in [swap, final, count_c, near_east, near_west, full_east, full_west] + counts_x:
        copy.wait_send()


def scatter(regions, words, counts, box_counts, token_counts, loss_scale):
    vmem, smem = pl.BlockSpec(memory_space=pltpu.VMEM), pl.BlockSpec(memory_space=pltpu.SMEM)
    sems = lambda n: [pltpu.SemaphoreType.DMA((n,))] * 2
    return pl.pallas_call(
        scatter_kernel,
        out_shape=(
            jax.ShapeDtypeStruct((2, BOX, D), BF),
            jax.ShapeDtypeStruct((2, TOK, D), BF),
        ),
        in_specs=[smem] * 3 + [vmem] * 3,
        out_specs=(vmem, vmem),
        scratch_shapes=[
            pltpu.VMEM((2, 8, 128), F32),
            pltpu.VMEM((8, 128), F32),
            pltpu.VMEM((3, 8, 128), F32),
            pltpu.VMEM((NZ - 1, 8, 128), F32),
            pltpu.VMEM((TOKS, HALF), BF),
            pltpu.VMEM((TOKS, HALF), BF),
            pltpu.VMEM((TOKS, HALF), F32),
            pltpu.VMEM((8, RB, D), BF),
            pltpu.VMEM((8, RB, D), BF),
            pltpu.VMEM((4, XB, HALF), BF),
            pltpu.VMEM((4, XB, HALF), BF),
            pltpu.VMEM((XB, HALF), F32),
            pltpu.VMEM(((NZ - 1) * CB, HALF), BF),
            pltpu.VMEM((24, HALF), F32),
            pltpu.VMEM((24, HALF), F32),
        ]
        + sems(8) + sems(NZ - 1) + sems(4) + sems(2) + sems(3 + NZ),
        compiler_params=pltpu.CompilerParams(
            collective_id=1, has_side_effects=True, vmem_limit_bytes=48 * 2**20
        ),
        name="scatter",
    )(box_counts, token_counts, loss_scale.reshape(1), regions, words, counts)


def on_device(
    regions,
    words,
    box_counts,
    token_counts,
    span_begin,
    span_length,
    bias_weight,
    logit_bias,
    loss_scale,
):
    rows, toks = gather(regions, words, box_counts, token_counts, span_length)
    region_sum, word_sum, counts = compute(rows, toks, bias_weight, logit_bias, span_begin, span_length)
    return scatter(region_sum, word_sum, counts, box_counts, token_counts, loss_scale)


def solution(mesh):
    in_specs = (
        P("dp", "text", None),
        P("dp", "text", None),
        P("dp"),
        P("dp"),
        P("dp", "text"),
        P("dp", "text"),
        P(),
        P(),
        P(),
    )
    out_specs = (P("dp", "text", None), P("dp", "text", None))
    return jax.shard_map(
        on_device, mesh=mesh, in_specs=in_specs, out_specs=out_specs, check_vma=False
    )
```

```python
import math

import jax
import jax.numpy as jnp
from jax import lax
from jax.experimental import pallas as pl
from jax.experimental.pallas import tpu as pltpu
from jax.sharding import PartitionSpec as P

MESH = pl.DeviceIdType.MESH
NX, NY, NZ = 4, 8, 12
D = 256
HALF = 128
BOX = 75
BOXP = 80
RB = 2 * BOXP
TOK = 12
OWN = 2 * TOK
CB = 2 * OWN
GROUP = NZ * OWN
NEAR = 7
SHIFT = 3
SIDE = NY * RB
ROWS = 2 * SIDE
BF = jnp.bfloat16
F32 = jnp.float32
LOG2E = math.log2(math.e)
Z_ORDER = (1, 11, 2, 10, 3, 9, 4, 8, 5, 7, 6)
Z_NEAR = Z_ORDER[:6]
Z_FAR = Z_ORDER[6:]
Y_ORDER = (1, 7, 2, 6, 3, 5, 4)
TILES = ((0, 0), (0, 1), (1, 1), (3, 1), (2, 1), (2, 0), (3, 0), (1, 0))


def iota(shape, dim):
    return lax.broadcasted_iota(jnp.int32, shape, dim)


def negative_slope(score):
    grown = jnp.exp2(score)
    total = 1.0 + grown
    rest = 1.0 / total
    prob = grown * rest
    lost = jnp.log(total) + (grown - (total - 1.0))
    return prob * prob * (0.5 * prob + rest * lost)


def positive_slope(score):
    small = jnp.exp2(-jnp.abs(score))
    total = 1.0 + small
    part = 1.0 / total
    prob = jnp.where(score >= 0.0, part, small * part)
    rest = jnp.where(score >= 0.0, small * part, part)
    lost = jnp.log(total) + (small - (total - 1.0)) + jnp.maximum(-score, 0.0) * math.log(2.0)
    return (-1.0 / 6.0) * rest * rest * (2.0 * prob * lost + rest)


def kernel(
    regions, words, box_hbm, token_hbm, begin_hbm, length_hbm, bias_hbm, logit_hbm, scale_hbm,
    region_out, word_out,
    box, token, logit, scale, begin, length, bias,
    wide, rows, rows_t, limit, toks, w, wt, offset, g, wp, csum, rp,
    twin_out, twin_in, y_out, y_in, y_own, x_out, x_in, z_out, z_in,
    tally, tally_x, tally_z,
    l_sem, y_send, y_recv, z_send, z_recv, x_send, x_recv, c_send, c_recv, n_send, n_recv,
    ry_send, ry_recv, rx_send, rx_recv, rz_send, rz_recv,
):
    dp = lax.axis_index("dp")
    z = lax.axis_index("text")
    x, y, c = dp // (NY * 2), (dp // 2) % NY, dp % 2

    def at_x(k):
        return (((x + k) % NX) * NY + y) * 2 + c, z

    def at_y(k):
        return (x * NY + (y + k) % NY) * 2 + c, z

    def at_z(k):
        return dp, (z + k) % NZ

    twin = ((x * NY + y) * 2 + 1 - c, z)

    def send(src, dst, sends, recvs, k, dev):
        return pltpu.make_async_remote_copy(
            src_ref=src, dst_ref=dst, send_sem=sends.at[k], recv_sem=recvs.at[k], device_id=dev, device_id_type=MESH
        )

    staged = (
        (box_hbm, box), (token_hbm, token), (begin_hbm, begin), (length_hbm, length), (bias_hbm, bias),
        (logit_hbm, logit), (scale_hbm, scale),
    )
    loads = [pltpu.make_async_copy(src, dst, l_sem.at[k]) for k, (src, dst) in enumerate(staged)]
    for load in loads:
        load.start()
    barrier = pltpu.get_barrier_semaphore()
    peers = [at_z(k) for k in Z_ORDER] + [at_y(k) for k in Y_ORDER] + [at_x(k) for k in (1, 3, 2)] + [twin]
    for dev in peers:
        pl.semaphore_signal(barrier, inc=1, device_id=dev, device_id_type=MESH)
    for load in loads:
        load.wait()

    tok = iota((TOK, D), 0)
    for cap in range(2):
        value = words[cap].astype(F32)
        wide[cap * TOK : (cap + 1) * TOK, :] = jnp.where(TOK * z + tok < token[cap], value, 0.0)
    mine = wide[0:OWN, :]
    toks[0, SHIFT] = jnp.concatenate([mine[:, 0:HALF], mine[:, HALF:D]], axis=0).astype(BF)

    count = jnp.zeros((1, 1), F32)
    for img in range(2):
        valid = BOX * z + iota((1, BOX), 1) < box[img]
        count = count + jnp.sum(jnp.where(valid, length[img : img + 1, :], 0).astype(F32), axis=1, keepdims=True)
    high = jnp.floor(count * (1.0 / 16.0))
    low = count - 16.0 * high
    lane, row = iota((BOXP, D), 1), iota((BOXP, D), 0)
    slot = jnp.where(lane < BOXP, lane, lane - BOXP)
    flag = (slot < BOX) & (lane < RB) & (BOX * z + slot < jnp.where(lane < BOXP, box[0], box[1]))
    for img in range(2):
        wide[img * BOXP + BOXP - 8 : (img + 1) * BOXP, :] = jnp.zeros((8, D), F32)
        wide[img * BOXP : img * BOXP + BOX, :] = regions[img].astype(F32)
        value = wide[img * BOXP : (img + 1) * BOXP, :]
        value = jnp.where((row < BOX) & (BOX * z + row < box[img]), value, 0.0)
        if img == 0:
            value = jnp.where((row == BOX) & flag, 1.0, value)
            value = jnp.where((row == BOX + 1) & (lane == 0), high, value)
            value = jnp.where((row == BOX + 1) & (lane == 1), low, value)
        rows[img * BOXP : (img + 1) * BOXP, :] = value.astype(BF)

    pl.semaphore_wait(barrier, len(peers))

    def block(r):
        return rows.at[pl.ds(r * RB, RB)]

    z_copies = {
        k: send(toks.at[0, SHIFT], toks.at[0, (SHIFT - k) % NZ], z_send, z_recv, k - 1, at_z(k)) for k in Z_ORDER
    }
    y_copies = {k: send(block(0), block(NY - k), y_send, y_recv, k - 1, at_y(k)) for k in Y_ORDER}
    twins = {r: send(block(r), block(NY + r), c_send, c_recv, r, twin) for r in range(NY)}
    near, far = pl.ds(0, NEAR), pl.ds(NEAR, NZ - NEAR)
    x_near = {k: send(toks.at[0, near], toks.at[NX - k, near], x_send, x_recv, k - 1, at_x(k)) for k in (2, 1, 3)}
    x_far = {k: send(toks.at[0, far], toks.at[NX - k, far], x_send, x_recv, 2 + k, at_x(k)) for k in (2, 1, 3)}
    for k in Z_ORDER:
        z_copies[k].start()
    for k in Y_ORDER:
        y_copies[k].start()
    twins[0].start()
    for k in Z_NEAR:
        z_copies[k].wait_recv()
    for copy in x_near.values():
        copy.start()
    for k in Y_ORDER[:4]:
        y_copies[k].wait_recv()
        twins[NY - k].start()
    for k in Z_FAR:
        z_copies[k].wait_recv()
    for copy in x_far.values():
        copy.start()
    for k in Y_ORDER[4:]:
        y_copies[k].wait_recv()
        twins[NY - k].start()

    def open_side(side):
        total = jnp.zeros((1, 1), F32)
        span = slice(side * SIDE, (side + 1) * SIDE)
        rows_t[:, span] = jnp.transpose(rows[span, :])
        for r in range(side * NY, (side + 1) * NY):
            info = rows[r * RB + BOXP - 16 : r * RB + BOXP, :].astype(F32)
            flags = info[BOX - BOXP + 16 : BOX - BOXP + 17, 0:RB]
            limit[0:1, r * RB : (r + 1) * RB] = jnp.where(flags > 0.5, 100.0, -1000.0)
            count = info[BOX - BOXP + 17 : BOX - BOXP + 18, :]
            total = total + 16.0 * count[:, 0:1] + count[:, 1:2]
        return total

    bias_row = bias[...]
    logit_value = logit[0]

    def open_group(r):
        value = toks[r].astype(F32).reshape(NZ, 2, OWN, HALF)
        value = jnp.concatenate([value[:, 0].reshape(GROUP, HALF), value[:, 1].reshape(GROUP, HALF)], axis=1)
        w[r] = value.astype(BF)
        wt[r] = jnp.transpose(value).astype(BF)
        column = (jnp.sum(value * bias_row, axis=1, keepdims=True) + logit_value) * LOG2E
        offset[r] = jnp.broadcast_to(column, (GROUP, HALF))

    def line(ref, missing):
        pad = jnp.full((1, BOXP - BOX), missing, jnp.int32)
        rest = jnp.full((1, D - RB), missing, jnp.int32)
        return jnp.concatenate([ref[0:1, :], pad, ref[1:2, :], pad, rest], axis=1)

    def score_tile(r, side):
        span = slice(side * SIDE, (side + 1) * SIDE)
        raw = jnp.dot(w[r], rows_t[:, span], preferred_element_type=F32)
        score = jnp.minimum(raw * (LOG2E / 16.0) + offset[r][:, 0:1], limit[0:1, span])
        slope = negative_slope(score)
        if r == 0 and side == 0:
            start = line(begin, 1 << 20)
            stop = start + line(length, 0)
            index = iota((GROUP, D), 0)
            token_index = ((z + index // OWN + (NZ - SHIFT)) % NZ) * TOK + index % TOK
            image = (iota((GROUP, D), 1) >= BOXP).astype(jnp.int32)
            positive = (image == (index // TOK) % 2) & (token_index >= start) & (token_index < stop)
            positive = positive & (limit[0:1, 0:D] > 0.0)
            first = jnp.where(positive, positive_slope(score[:, 0:D]), slope[:, 0:D])
            slope = jnp.concatenate([first, slope[:, D:SIDE]], axis=1)
        total = slope[:, 0:HALF]
        for q in range(1, SIDE // HALF):
            total = total + slope[:, q * HALF : (q + 1) * HALF]
        g[side] = slope.astype(BF)
        return total

    def sum_tile(r, side, total, first_of_group, first_of_side):
        span = slice(side * SIDE, (side + 1) * SIDE)
        grads = jnp.dot(g[side], rows[span, :], preferred_element_type=F32)
        if first_of_group:
            wp[r] = grads
            csum[r] = total
        else:
            wp[r] = wp[r] + grads
            csum[r] = csum[r] + total
        part = jnp.dot(wt[r], g[side], preferred_element_type=F32)
        if first_of_side:
            rp[side] = part
        else:
            rp[side] = rp[side] + part

    def close_group(r):
        column = jnp.sum(csum[r], axis=1, keepdims=True)
        return wp[r] + column * (16.0 * bias_row)

    rx_copies = {k: send(x_out.at[k - 1], x_in.at[k - 1], rx_send, rx_recv, k - 1, at_x(k)) for k in (1, 2, 3)}
    twin_copy = send(twin_out, twin_in, c_send, c_recv, NY, twin)
    n_x = {k: send(tally.at[0], tally_x.at[k - 1], n_send, n_recv, k - 1, at_x(k)) for k in (1, 3, 2)}
    n_z = {k: send(tally.at[1], tally_z.at[k - 1], n_send, n_recv, 2 + k, at_z(k)) for k in Z_ORDER}

    counts = open_side(0)
    open_group(0)
    groups, sides = set(), set()
    for r, side in TILES:
        if (r, side) == (0, 1):
            for k in range(NY):
                twins[k].wait_recv()
            counts = counts + open_side(1)
            tally[0] = jnp.broadcast_to(counts, (8, HALF))
            for copy in n_x.values():
                copy.start()
        if r not in groups and r != 0:
            x_near[NX - r].wait_recv()
            x_far[NX - r].wait_recv()
            open_group(r)
        total = score_tile(r, side)
        sum_tile(r, side, total, r not in groups, side not in sides)
        if r in groups and r != 0:
            x_out[r - 1] = close_group(r).astype(BF)
            rx_copies[r].start()
        if (r, side) == (1, 1):
            for copy in n_x.values():
                copy.wait_recv()
            tally[1] = tally[0] + tally_x[0] + tally_x[1] + tally_x[2]
            for copy in n_z.values():
                copy.start()
        if (r, side) == (2, 1):
            twin_out[...] = jnp.transpose(rp[1]).astype(BF)
            twin_copy.start()
        groups.add(r)
        sides.add(side)

    twin_copy.wait_recv()
    ry_copies = {k: send(y_out.at[k - 1], y_in.at[k - 1], ry_send, ry_recv, k - 1, at_y(k)) for k in Y_ORDER}
    both = jnp.transpose(rp[0]) + twin_in[...].astype(F32)
    y_own[...] = both[0:RB, :]
    for k in (4, 3, 5, 2, 6, 1, 7):
        y_out[k - 1] = both[k * RB : (k + 1) * RB, :].astype(BF)
        ry_copies[k].start()

    sums = close_group(0)
    for k in (3, 2, 1):
        rx_copies[k].wait_recv()
        sums = sums + x_in[k - 1].astype(F32)
    sums = sums.reshape(NZ, OWN, D)
    halves = jnp.concatenate([sums[:, :, 0:HALF], sums[:, :, HALF:D]], axis=1)
    z_out[...] = halves.astype(BF)
    rz_copies = {
        k: send(z_out.at[(SHIFT + k) % NZ], z_in.at[k - 1], rz_send, rz_recv, k - 1, at_z(k)) for k in Z_ORDER
    }
    for k in reversed(Z_ORDER):
        rz_copies[k].start()
    chip = halves[SHIFT]

    positives = tally[1]
    for k in Z_ORDER:
        n_z[k].wait_recv()
        positives = positives + tally_z[k - 1]
    coef = (scale[0] * (1.5 / 16.0)) / positives[0:1, 0:1]

    for k in Z_ORDER:
        rz_copies[k].wait_recv()
        chip = chip + z_in[k - 1].astype(F32)
    value = jnp.concatenate([chip[0:OWN], chip[OWN:CB]], axis=1) * coef
    for cap in range(2):
        part = value[cap * TOK : (cap + 1) * TOK]
        word_out[cap] = jnp.where(TOK * z + tok < token[cap], part, 0.0).astype(BF)

    both = y_own[...]
    for k in Y_ORDER:
        ry_copies[k].wait_recv()
        both = both + y_in[k - 1].astype(F32)
    for img in range(2):
        part = both[img * BOXP : (img + 1) * BOXP] * coef
        part = jnp.where(BOX * z + row < box[img], part, 0.0)
        region_out[img] = part[0:BOX].astype(BF)

    for copies in (z_copies, y_copies, twins, x_near, x_far, rx_copies, n_x, n_z, ry_copies, rz_copies):
        for copy in copies.values():
            copy.wait_send()
    twin_copy.wait_send()


def on_device(
    regions,
    words,
    box_counts,
    token_counts,
    span_begin,
    span_length,
    bias_weight,
    logit_bias,
    loss_scale,
):
    vmem, any_place = pl.BlockSpec(memory_space=pltpu.VMEM), pl.BlockSpec(memory_space=pl.ANY)
    smem = pltpu.SMEM
    hold = pltpu.VMEM

    def sems(n):
        return [pltpu.SemaphoreType.DMA((n,))] * 2

    return pl.pallas_call(
        kernel,
        out_shape=(
            jax.ShapeDtypeStruct((2, BOX, D), BF),
            jax.ShapeDtypeStruct((2, TOK, D), BF),
        ),
        in_specs=[vmem] * 2 + [any_place] * 7,
        out_specs=(vmem, vmem),
        scratch_shapes=[
            smem((2,), jnp.int32),
            smem((2,), jnp.int32),
            smem((1,), F32),
            smem((1,), F32),
            hold((2, BOX), jnp.int32),
            hold((2, BOX), jnp.int32),
            hold((1, D), F32),
            hold((RB, D), F32),
            hold((ROWS, D), BF),
            hold((D, ROWS), BF),
            hold((8, ROWS), F32),
            hold((NX, NZ, CB, HALF), BF),
            hold((NX, GROUP, D), BF),
            hold((NX, D, GROUP), BF),
            hold((NX, GROUP, HALF), F32),
            hold((2, GROUP, SIDE), BF),
            hold((NX, GROUP, D), F32),
            hold((NX, GROUP, HALF), F32),
            hold((2, D, SIDE), F32),
            hold((SIDE, D), BF),
            hold((SIDE, D), BF),
            hold((NY - 1, RB, D), BF),
            hold((NY - 1, RB, D), BF),
            hold((RB, D), F32),
            hold((NX - 1, GROUP, D), BF),
            hold((NX - 1, GROUP, D), BF),
            hold((NZ, CB, HALF), BF),
            hold((NZ - 1, CB, HALF), BF),
            hold((2, 8, HALF), F32),
            hold((NX - 1, 8, HALF), F32),
            hold((NZ - 1, 8, HALF), F32),
            pltpu.SemaphoreType.DMA((7,)),
        ]
        + sems(NY - 1) + sems(NZ - 1) + sems(6) + sems(NY + 1) + sems(NX + NZ - 2)
        + sems(NY - 1) + sems(NX - 1) + sems(NZ - 1),
        compiler_params=pltpu.CompilerParams(
            collective_id=0, has_side_effects=True, vmem_limit_bytes=56 * 2**20
        ),
        name="alignment",
    )(
        regions, words, box_counts, token_counts, span_begin, span_length,
        bias_weight.reshape(1, D), logit_bias.reshape(1), loss_scale.reshape(1),
    )


def solution(mesh):
    in_specs = (
        P("dp", "text", None),
        P("dp", "text", None),
        P("dp"),
        P("dp"),
        P("dp", "text"),
        P("dp", "text"),
        P(),
        P(),
        P(),
    )
    out_specs = (P("dp", "text", None), P("dp", "text", None))
    return jax.shard_map(
        on_device, mesh=mesh, in_specs=in_specs, out_specs=out_specs, check_vma=False
    )
```

```python
import math

import jax
import jax.numpy as jnp
from jax import lax
from jax.experimental import pallas as pl
from jax.experimental.pallas import tpu as pltpu
from jax.sharding import PartitionSpec as P

MESH = pl.DeviceIdType.MESH
NX, NY, NZ = 4, 8, 12
D = 256
HALF = 128
BOX = 75
BOXP = 80
RB = 2 * BOXP
TOK = 12
OWN = 2 * TOK
CB = 2 * OWN
GROUP = NZ * OWN
NEAR = 7
SHIFT = 3
SIDE = NY * RB
ROWS = 2 * SIDE
BF = jnp.bfloat16
F32 = jnp.float32
LOG2E = math.log2(math.e)
Z_ORDER = (1, 11, 2, 10, 3, 9, 4, 8, 5, 7, 6)
Z_NEAR = Z_ORDER[:6]
Z_FAR = Z_ORDER[6:]
Y_SIDES = ((0, 1, 7, 2), (6, 5, 3, 4))
PART = len(Y_SIDES[0]) * RB


def iota(shape, dim):
    return lax.broadcasted_iota(jnp.int32, shape, dim)


def negative_slope(score):
    grown = jnp.exp2(score)
    total = 1.0 + grown
    rest = 1.0 / total
    prob = grown * rest
    lost = jnp.log(total) + (grown - (total - 1.0))
    return prob * prob * (0.5 * prob + rest * lost)


def positive_slope(score):
    small = jnp.exp2(-jnp.abs(score))
    total = 1.0 + small
    part = 1.0 / total
    prob = jnp.where(score >= 0.0, part, small * part)
    rest = jnp.where(score >= 0.0, small * part, part)
    lost = jnp.log(total) + (small - (total - 1.0)) + jnp.maximum(-score, 0.0) * math.log(2.0)
    return (-1.0 / 6.0) * rest * rest * (2.0 * prob * lost + rest)


def kernel(
    regions, words, box_hbm, token_hbm, begin_hbm, length_hbm, bias_hbm, logit_hbm, scale_hbm,
    region_out, word_out,
    box, token, logit, scale, begin, length, bias,
    wide, rows, rows_t, limit, toks, w, wt, offset, g, wp, csum, rp,
    twin_out, twin_in, y_out, y_in, y_own, x_out, x_in, z_out, z_in,
    tally, tally_x, tally_z,
    l_sem, y_send, y_recv, z_send, z_recv, x_send, x_recv, c_send, c_recv, n_send, n_recv,
    ry_send, ry_recv, rx_send, rx_recv, rz_send, rz_recv,
):
    dp = lax.axis_index("dp")
    z = lax.axis_index("text")
    x, y, c = dp // (NY * 2), (dp // 2) % NY, dp % 2

    def at_x(k):
        return (((x + k) % NX) * NY + y) * 2 + c, z

    def at_y(k):
        return (x * NY + (y + k) % NY) * 2 + c, z

    def at_z(k):
        return dp, (z + k) % NZ

    twin = ((x * NY + y) * 2 + 1 - c, z)

    def send(src, dst, sends, recvs, k, dev):
        return pltpu.make_async_remote_copy(
            src_ref=src, dst_ref=dst, send_sem=sends.at[k], recv_sem=recvs.at[k], device_id=dev, device_id_type=MESH
        )

    barrier = pltpu.get_barrier_semaphore()
    peers = [at_z(k) for k in Z_ORDER] + [at_y(k) for k in (1, 7, 2, 6)] + [at_x(k) for k in (1, 3, 2)] + [twin]
    for dev in peers:
        pl.semaphore_signal(barrier, inc=1, device_id=dev, device_id_type=MESH)
    staged = (
        (box_hbm, box), (token_hbm, token), (begin_hbm, begin), (length_hbm, length), (bias_hbm, bias),
        (logit_hbm, logit), (scale_hbm, scale),
    )
    loads = [pltpu.make_async_copy(src, dst, l_sem.at[k]) for k, (src, dst) in enumerate(staged)]
    for load in loads:
        load.start()
    for load in loads:
        load.wait()

    tok = iota((TOK, D), 0)
    for cap in range(2):
        value = words[cap].astype(F32)
        wide[cap * TOK : (cap + 1) * TOK, :] = jnp.where(TOK * z + tok < token[cap], value, 0.0)
    mine = wide[0:OWN, :]
    toks[0, SHIFT] = jnp.concatenate([mine[:, 0:HALF], mine[:, HALF:D]], axis=0).astype(BF)

    count = jnp.zeros((1, 1), F32)
    for img in range(2):
        valid = BOX * z + iota((1, BOX), 1) < box[img]
        count = count + jnp.sum(jnp.where(valid, length[img : img + 1, :], 0).astype(F32), axis=1, keepdims=True)
    high = jnp.floor(count * (1.0 / 16.0))
    low = count - 16.0 * high
    lane, row = iota((BOXP, D), 1), iota((BOXP, D), 0)
    slot = jnp.where(lane < BOXP, lane, lane - BOXP)
    flag = (slot < BOX) & (lane < RB) & (BOX * z + slot < jnp.where(lane < BOXP, box[0], box[1]))
    for img in range(2):
        wide[img * BOXP + BOXP - 8 : (img + 1) * BOXP, :] = jnp.zeros((8, D), F32)
        wide[img * BOXP : img * BOXP + BOX, :] = regions[img].astype(F32)
        value = wide[img * BOXP : (img + 1) * BOXP, :]
        value = jnp.where((row < BOX) & (BOX * z + row < box[img]), value, 0.0)
        if img == 0:
            value = jnp.where((row == BOX) & flag, 1.0, value)
            value = jnp.where((row == BOX + 1) & (lane == 0), high, value)
            value = jnp.where((row == BOX + 1) & (lane == 1), low, value)
        rows[img * BOXP : (img + 1) * BOXP, :] = value.astype(BF)

    pl.semaphore_wait(barrier, len(peers))

    def where(r, other):
        side = 0 if r in Y_SIDES[0] else 1
        return (side * 2 + other) * PART + Y_SIDES[side].index(r) * RB

    def block(r, other=0):
        return rows.at[pl.ds(where(r, other), RB)]

    z_copies = {
        k: send(toks.at[0, SHIFT], toks.at[0, (SHIFT - k) % NZ], z_send, z_recv, k - 1, at_z(k)) for k in Z_ORDER
    }
    def half(r, k):
        return rows.at[pl.ds(where(r, 0) + k * BOXP, BOXP)]

    y_copies = {
        r: send(block(0), block(r), y_send, y_recv, k, at_y(NY - r)) for k, r in enumerate((7, 1, 6, 2))
    }
    y_copies[5] = send(block(6), block(5), y_send, y_recv, 4, at_y(1))
    y_copies[3] = send(block(2), block(3), y_send, y_recv, 5, at_y(7))
    y_copies[4] = send(half(6, 0), half(4, 0), y_send, y_recv, 6, at_y(2))
    y_copies[8] = send(half(2, 1), half(4, 1), y_send, y_recv, 7, at_y(6))
    twins = {r: send(block(r), block(r, 1), c_send, c_recv, r, twin) for r in range(NY)}
    near, far = pl.ds(0, NEAR), pl.ds(NEAR, NZ - NEAR)
    x_near = {k: send(toks.at[0, near], toks.at[NX - k, near], x_send, x_recv, k - 1, at_x(k)) for k in (2, 1, 3)}
    x_far = {k: send(toks.at[0, far], toks.at[NX - k, far], x_send, x_recv, 2 + k, at_x(k)) for k in (2, 1, 3)}
    for k in Z_ORDER:
        z_copies[k].start()
    for r in (7, 1, 6, 2):
        y_copies[r].start()
    twins[0].start()
    for k in Z_NEAR:
        z_copies[k].wait_recv()
    for copy in x_near.values():
        copy.start()

    def pass_on(r, onward=()):
        y_copies[r].wait_recv()
        for k in onward:
            y_copies[k].start()
        twins[r].start()

    pass_on(7)
    pass_on(1)
    pass_on(6, (5, 4))
    pass_on(2, (3, 8))
    for k in Z_FAR:
        z_copies[k].wait_recv()
    for copy in x_far.values():
        copy.start()

    def open_side(side):
        for r in Y_SIDES[side]:
            twins[r].wait_recv()
        total = jnp.zeros((1, 1), F32)
        span = slice(side * SIDE, (side + 1) * SIDE)
        rows_t[:, span] = jnp.transpose(rows[span, :])
        for r in range(side * NY, (side + 1) * NY):
            info = rows[r * RB + BOXP - 16 : r * RB + BOXP, :].astype(F32)
            flags = info[BOX - BOXP + 16 : BOX - BOXP + 17, 0:RB]
            limit[0:1, r * RB : (r + 1) * RB] = jnp.where(flags > 0.5, 100.0, -1000.0)
            count = info[BOX - BOXP + 17 : BOX - BOXP + 18, :]
            total = total + 16.0 * count[:, 0:1] + count[:, 1:2]
        return total

    bias_row = bias[...]
    logit_value = logit[0]

    def open_group(r):
        value = toks[r].astype(F32).reshape(NZ, 2, OWN, HALF)
        value = jnp.concatenate([value[:, 0].reshape(GROUP, HALF), value[:, 1].reshape(GROUP, HALF)], axis=1)
        w[r] = value.astype(BF)
        wt[r] = jnp.transpose(value).astype(BF)
        column = (jnp.sum(value * bias_row, axis=1, keepdims=True) + logit_value) * LOG2E
        offset[r] = jnp.broadcast_to(column, (GROUP, HALF))

    def line(ref, missing):
        pad = jnp.full((1, BOXP - BOX), missing, jnp.int32)
        rest = jnp.full((1, D - RB), missing, jnp.int32)
        return jnp.concatenate([ref[0:1, :], pad, ref[1:2, :], pad, rest], axis=1)

    def score_tile(r, side):
        span = slice(side * SIDE, (side + 1) * SIDE)
        raw = jnp.dot(w[r], rows_t[:, span], preferred_element_type=F32)
        score = jnp.minimum(raw * (LOG2E / 16.0) + offset[r][:, 0:1], limit[0:1, span])
        slope = negative_slope(score)
        if r == 0 and side == 0:
            start = line(begin, 1 << 20)
            stop = start + line(length, 0)
            index = iota((GROUP, D), 0)
            token_index = ((z + index // OWN + (NZ - SHIFT)) % NZ) * TOK + index % TOK
            image = (iota((GROUP, D), 1) >= BOXP).astype(jnp.int32)
            positive = (image == (index // TOK) % 2) & (token_index >= start) & (token_index < stop)
            positive = positive & (limit[0:1, 0:D] > 0.0)
            first = jnp.where(positive, positive_slope(score[:, 0:D]), slope[:, 0:D])
            slope = jnp.concatenate([first, slope[:, D:SIDE]], axis=1)
        total = slope[:, 0:HALF]
        for q in range(1, SIDE // HALF):
            total = total + slope[:, q * HALF : (q + 1) * HALF]
        g[side] = slope.astype(BF)
        return total

    def sum_tile(r, side, total, first_of_group, first_of_side):
        span = slice(side * SIDE, (side + 1) * SIDE)
        grads = jnp.dot(g[side], rows[span, :], preferred_element_type=F32)
        if first_of_group:
            wp[r] = grads
            csum[r] = total
        else:
            wp[r] = wp[r] + grads
            csum[r] = csum[r] + total
        part = jnp.dot(wt[r], g[side], preferred_element_type=F32)
        if first_of_side:
            rp[side] = part
        else:
            rp[side] = rp[side] + part

    def close_group(r):
        column = jnp.sum(csum[r], axis=1, keepdims=True)
        return wp[r] + column * (16.0 * bias_row)

    rx_copies = {k: send(x_out.at[k - 1], x_in.at[k - 1], rx_send, rx_recv, k - 1, at_x(k)) for k in (1, 2, 3)}
    ry_copies = {
        r: send(y_out.at[k], y_in.at[k], ry_send, ry_recv, k, at_y(to))
        for k, (r, to) in enumerate(((1, 1), (7, 7), (3, 1), (5, 7), (2, 2), (6, 6)))
    }
    upper, lower = pl.ds(0, BOXP), pl.ds(BOXP, BOXP)
    ry_copies[4] = send(y_out.at[6, upper], y_in.at[6, upper], ry_send, ry_recv, 6, at_y(2))
    ry_copies[8] = send(y_out.at[6, lower], y_in.at[6, lower], ry_send, ry_recv, 7, at_y(6))
    twin_copies = {
        side: send(twin_out.at[side], twin_in.at[side], c_send, c_recv, NY + side, twin) for side in range(2)
    }
    n_x = {k: send(tally.at[0], tally_x.at[k - 1], n_send, n_recv, k - 1, at_x(k)) for k in (1, 3, 2)}
    n_z = {k: send(tally.at[1], tally_z.at[k - 1], n_send, n_recv, 2 + k, at_z(k)) for k in Z_ORDER}

    def tile(r, side):
        total = score_tile(r, side)
        sum_tile(r, side, total, (r, side) in ((0, 0), (1, 0), (2, 0), (3, 1)), (r, side) in ((0, 0), (2, 1)))

    def words_of(r):
        x_near[NX - r].wait_recv()
        x_far[NX - r].wait_recv()
        open_group(r)

    def send_words(r):
        x_out[r - 1] = close_group(r).astype(BF)
        rx_copies[r].start()

    def other_core(side):
        twin_out[side] = jnp.transpose(rp[side][:, PART:SIDE]).astype(BF)
        twin_copies[side].start()

    def to_owners(side):
        twin_copies[side].wait_recv()
        both = jnp.transpose(rp[side][:, 0:PART]) + twin_in[side].astype(F32)
        kept = {0: 0, 2: 1, 6: 2}
        slots = {1: 0, 7: 1, 3: 2, 5: 3, 4: 6}
        for k, r in reversed(tuple(enumerate(Y_SIDES[side]))):
            part = both[k * RB : (k + 1) * RB, :]
            if r in kept:
                y_own[kept[r]] = part
            else:
                y_out[slots[r]] = part.astype(BF)
                ry_copies[r].start()
                if r == 4:
                    ry_copies[8].start()

    def pass_sums():
        for r, kept, near, far, part in ((2, 1, 3, 4, upper), (6, 2, 5, 8, lower)):
            slot, k = {2: 4, 6: 5}[r], {3: 2, 5: 3}[near]
            ry_copies[near].wait_recv()
            ry_copies[far].wait_recv()
            y_own[kept] = y_own[kept] + y_in[k].astype(F32)
            y_own[kept, part, :] = y_own[kept, part, :] + y_in[6, part, :].astype(F32)
            y_out[slot] = y_own[kept].astype(BF)
            ry_copies[r].start()

    open_group(0)
    counts = open_side(0)
    tile(0, 0)
    pass_on(5)
    pass_on(3)
    words_of(1)
    tile(1, 0)
    y_copies[8].wait_recv()
    pass_on(4)
    words_of(2)
    tile(2, 0)
    counts = counts + open_side(1)
    tally[0] = jnp.broadcast_to(counts, (8, HALF))
    for copy in n_x.values():
        copy.start()
    tile(2, 1)
    send_words(2)
    tile(0, 1)
    words_of(3)
    tile(1, 1)
    send_words(1)
    for copy in n_x.values():
        copy.wait_recv()
    tally[1] = tally[0] + tally_x[0] + tally_x[1] + tally_x[2]
    for copy in n_z.values():
        copy.start()
    tile(3, 1)
    other_core(1)
    tile(3, 0)
    other_core(0)
    send_words(3)
    to_owners(1)
    to_owners(0)

    sums = close_group(0)
    for k in (2, 1, 3):
        rx_copies[k].wait_recv()
        sums = sums + x_in[k - 1].astype(F32)
    sums = sums.reshape(NZ, OWN, D)
    halves = jnp.concatenate([sums[:, :, 0:HALF], sums[:, :, HALF:D]], axis=1)
    z_out[...] = halves.astype(BF)
    rz_copies = {
        k: send(z_out.at[(SHIFT + k) % NZ], z_in.at[k - 1], rz_send, rz_recv, k - 1, at_z(k)) for k in Z_ORDER
    }
    for k in reversed(Z_ORDER):
        rz_copies[k].start()
    chip = halves[SHIFT]
    pass_sums()

    positives = tally[1]
    for k in Z_ORDER:
        n_z[k].wait_recv()
        positives = positives + tally_z[k - 1]
    coef = (scale[0] * (1.5 / 16.0)) / positives[0:1, 0:1]

    for k in Z_ORDER:
        rz_copies[k].wait_recv()
        chip = chip + z_in[k - 1].astype(F32)
    value = jnp.concatenate([chip[0:OWN], chip[OWN:CB]], axis=1) * coef
    for cap in range(2):
        part = value[cap * TOK : (cap + 1) * TOK]
        word_out[cap] = jnp.where(TOK * z + tok < token[cap], part, 0.0).astype(BF)

    both = y_own[0]
    for k, r in ((0, 1), (1, 7), (4, 2), (5, 6)):
        ry_copies[r].wait_recv()
        both = both + y_in[k].astype(F32)
    for img in range(2):
        part = both[img * BOXP : (img + 1) * BOXP] * coef
        part = jnp.where(BOX * z + row < box[img], part, 0.0)
        region_out[img] = part[0:BOX].astype(BF)

    for copies in (z_copies, y_copies, twins, x_near, x_far, rx_copies, n_x, n_z, ry_copies, rz_copies, twin_copies):
        for copy in copies.values():
            copy.wait_send()


def on_device(
    regions,
    words,
    box_counts,
    token_counts,
    span_begin,
    span_length,
    bias_weight,
    logit_bias,
    loss_scale,
):
    vmem, in_hbm = pl.BlockSpec(memory_space=pltpu.VMEM), pl.BlockSpec(memory_space=pltpu.HBM)
    smem = pltpu.SMEM
    hold = pltpu.VMEM

    def sems(n):
        return [pltpu.SemaphoreType.DMA((n,))] * 2

    return pl.pallas_call(
        kernel,
        out_shape=(
            jax.ShapeDtypeStruct((2, BOX, D), BF),
            jax.ShapeDtypeStruct((2, TOK, D), BF),
        ),
        in_specs=[vmem] * 2 + [in_hbm] * 7,
        out_specs=(vmem, vmem),
        scratch_shapes=[
            smem((2,), jnp.int32),
            smem((2,), jnp.int32),
            smem((1,), F32),
            smem((1,), F32),
            hold((2, BOX), jnp.int32),
            hold((2, BOX), jnp.int32),
            hold((1, D), F32),
            hold((RB, D), F32),
            hold((ROWS, D), BF),
            hold((D, ROWS), BF),
            hold((8, ROWS), F32),
            hold((NX, NZ, CB, HALF), BF),
            hold((NX, GROUP, D), BF),
            hold((NX, D, GROUP), BF),
            hold((NX, GROUP, HALF), F32),
            hold((2, GROUP, SIDE), BF),
            hold((NX, GROUP, D), F32),
            hold((NX, GROUP, HALF), F32),
            hold((2, D, SIDE), F32),
            hold((2, PART, D), BF),
            hold((2, PART, D), BF),
            hold((NY - 1, RB, D), BF),
            hold((NY - 1, RB, D), BF),
            hold((3, RB, D), F32),
            hold((NX - 1, GROUP, D), BF),
            hold((NX - 1, GROUP, D), BF),
            hold((NZ, CB, HALF), BF),
            hold((NZ - 1, CB, HALF), BF),
            hold((2, 8, HALF), F32),
            hold((NX - 1, 8, HALF), F32),
            hold((NZ - 1, 8, HALF), F32),
            pltpu.SemaphoreType.DMA((7,)),
        ]
        + sems(NY) + sems(NZ - 1) + sems(6) + sems(NY + 2) + sems(NX + NZ - 2)
        + sems(NY) + sems(NX - 1) + sems(NZ - 1),
        compiler_params=pltpu.CompilerParams(
            collective_id=0, has_side_effects=True, vmem_limit_bytes=32 * 2**20
        ),
        name="alignment",
    )(
        regions, words, box_counts, token_counts, span_begin, span_length,
        bias_weight.reshape(1, D), logit_bias.reshape(1), loss_scale.reshape(1),
    )


def solution(mesh):
    in_specs = (
        P("dp", "text", None),
        P("dp", "text", None),
        P("dp"),
        P("dp"),
        P("dp", "text"),
        P("dp", "text"),
        P(),
        P(),
        P(),
    )
    out_specs = (P("dp", "text", None), P("dp", "text", None))
    return jax.shard_map(
        on_device, mesh=mesh, in_specs=in_specs, out_specs=out_specs, check_vma=False
    )
```

```python
import math

import jax
import jax.numpy as jnp
from jax import lax
from jax.experimental import pallas as pl
from jax.experimental.pallas import tpu as pltpu
from jax.sharding import PartitionSpec as P

MESH = pl.DeviceIdType.MESH
NX, NY, NZ = 4, 8, 12
D = 256
HALF = 128
BOX = 75
BOXP = 80
RB = 2 * BOXP
TOK = 12
OWN = 2 * TOK
CB = 2 * OWN
GROUP = NZ * OWN
NEAR = 7
SHIFT = 3
SIDE = NY * RB
ROWS = 2 * SIDE
BF = jnp.bfloat16
F32 = jnp.float32
LOG2E = math.log2(math.e)
Z_ORDER = (1, 11, 2, 10, 3, 9, 4, 8, 5, 7, 6)
Z_NEAR = Z_ORDER[:6]
Z_FAR = Z_ORDER[6:]
Y_SIDES = ((0, 1, 7, 2), (6, 5, 3, 4))
GP = 384
PART = len(Y_SIDES[0]) * RB


def iota(shape, dim):
    return lax.broadcasted_iota(jnp.int32, shape, dim)


def negative_slope(score):
    grown = jnp.exp2(score)
    total = 1.0 + grown
    rest = 1.0 / total
    prob = grown * rest
    lost = jnp.log(total) + (grown - (total - 1.0))
    return prob * prob * (0.5 * prob + rest * lost)


def positive_slope(score):
    small = jnp.exp2(-jnp.abs(score))
    total = 1.0 + small
    part = 1.0 / total
    prob = jnp.where(score >= 0.0, part, small * part)
    rest = jnp.where(score >= 0.0, small * part, part)
    lost = jnp.log(total) + (small - (total - 1.0)) + jnp.maximum(-score, 0.0) * math.log(2.0)
    return (-1.0 / 6.0) * rest * rest * (2.0 * prob * lost + rest)


def kernel(
    regions, words, box_hbm, token_hbm, begin_hbm, length_hbm, bias_hbm, logit_hbm, scale_hbm,
    region_out, word_out,
    box, token, logit, scale, begin, length, bias,
    wide, rows, rows_t, limit, toks, w, wt, offset, g, wp, csum, rp,
    twin_out, twin_in, y_out, y_in, y_own, x_out, x_in, z_out, z_in,
    tally, tally_x, tally_z,
    l_sem, y_send, y_recv, z_send, z_recv, x_send, x_recv, c_send, c_recv, n_send, n_recv,
    ry_send, ry_recv, rx_send, rx_recv, rz_send, rz_recv,
):
    dp = lax.axis_index("dp")
    z = lax.axis_index("text")
    x, y, c = dp // (NY * 2), (dp // 2) % NY, dp % 2

    def at_x(k):
        return (((x + k) % NX) * NY + y) * 2 + c, z

    def at_y(k):
        return (x * NY + (y + k) % NY) * 2 + c, z

    def at_z(k):
        return dp, (z + k) % NZ

    twin = ((x * NY + y) * 2 + 1 - c, z)

    def send(src, dst, sends, recvs, k, dev):
        return pltpu.make_async_remote_copy(
            src_ref=src, dst_ref=dst, send_sem=sends.at[k], recv_sem=recvs.at[k], device_id=dev, device_id_type=MESH
        )

    barrier = pltpu.get_barrier_semaphore()
    peers = [at_z(k) for k in Z_ORDER] + [at_y(k) for k in (1, 7, 2, 6)] + [at_x(k) for k in (1, 3, 2)] + [twin]
    for dev in peers:
        pl.semaphore_signal(barrier, inc=1, device_id=dev, device_id_type=MESH)
    staged = (
        (box_hbm, box), (token_hbm, token), (begin_hbm, begin), (length_hbm, length), (bias_hbm, bias),
        (logit_hbm, logit), (scale_hbm, scale),
    )
    loads = [pltpu.make_async_copy(src, dst, l_sem.at[k]) for k, (src, dst) in enumerate(staged)]
    for load in loads:
        load.start()
    for load in loads:
        load.wait()

    tok = iota((TOK, D), 0)
    for cap in range(2):
        value = words[cap].astype(F32)
        wide[cap * TOK : (cap + 1) * TOK, :] = jnp.where(TOK * z + tok < token[cap], value, 0.0)
    mine = wide[0:OWN, :]
    toks[0, SHIFT] = jnp.concatenate([mine[:, 0:HALF], mine[:, HALF:D]], axis=0).astype(BF)

    count = jnp.zeros((1, 1), F32)
    for img in range(2):
        valid = BOX * z + iota((1, BOX), 1) < box[img]
        count = count + jnp.sum(jnp.where(valid, length[img : img + 1, :], 0).astype(F32), axis=1, keepdims=True)
    high = jnp.floor(count * (1.0 / 16.0))
    low = count - 16.0 * high
    lane, row = iota((BOXP, D), 1), iota((BOXP, D), 0)
    slot = jnp.where(lane < BOXP, lane, lane - BOXP)
    flag = (slot < BOX) & (lane < RB) & (BOX * z + slot < jnp.where(lane < BOXP, box[0], box[1]))
    for img in range(2):
        wide[img * BOXP + BOXP - 8 : (img + 1) * BOXP, :] = jnp.zeros((8, D), F32)
        wide[img * BOXP : img * BOXP + BOX, :] = regions[img].astype(F32)
        value = wide[img * BOXP : (img + 1) * BOXP, :]
        value = jnp.where((row < BOX) & (BOX * z + row < box[img]), value, 0.0)
        if img == 0:
            value = jnp.where((row == BOX) & flag, 1.0, value)
            value = jnp.where((row == BOX + 1) & (lane == 0), high, value)
            value = jnp.where((row == BOX + 1) & (lane == 1), low, value)
        rows[img * BOXP : (img + 1) * BOXP, :] = value.astype(BF)

    wt[...] = jnp.zeros_like(wt)
    for side in range(2):
        for r in range(NX):
            g[side, r // 2, r % 2 * GP + GROUP : (r % 2 + 1) * GP, :] = jnp.zeros((GP - GROUP, SIDE), BF)
    pl.semaphore_wait(barrier, len(peers))

    def where(r, other):
        side = 0 if r in Y_SIDES[0] else 1
        return (side * 2 + other) * PART + Y_SIDES[side].index(r) * RB

    def block(r, other=0):
        return rows.at[pl.ds(where(r, other), RB)]

    z_copies = {
        k: send(toks.at[0, SHIFT], toks.at[0, (SHIFT - k) % NZ], z_send, z_recv, k - 1, at_z(k)) for k in Z_ORDER
    }
    def half(r, k):
        return rows.at[pl.ds(where(r, 0) + k * BOXP, BOXP)]

    y_copies = {
        r: send(block(0), block(r), y_send, y_recv, k, at_y(NY - r)) for k, r in enumerate((7, 1, 6, 2))
    }
    y_copies[5] = send(block(6), block(5), y_send, y_recv, 4, at_y(1))
    y_copies[3] = send(block(2), block(3), y_send, y_recv, 5, at_y(7))
    y_copies[4] = send(half(6, 0), half(4, 0), y_send, y_recv, 6, at_y(2))
    y_copies[8] = send(half(2, 1), half(4, 1), y_send, y_recv, 7, at_y(6))
    twins = {r: send(block(r), block(r, 1), c_send, c_recv, r, twin) for r in range(NY)}
    near, far = pl.ds(0, NEAR), pl.ds(NEAR, NZ - NEAR)
    x_near = {k: send(toks.at[0, near], toks.at[NX - k, near], x_send, x_recv, k - 1, at_x(k)) for k in (2, 1, 3)}
    x_far = {k: send(toks.at[0, far], toks.at[NX - k, far], x_send, x_recv, 2 + k, at_x(k)) for k in (2, 1, 3)}
    for k in Z_ORDER:
        z_copies[k].start()
    for r in (7, 1, 6, 2):
        y_copies[r].start()
    twins[0].start()
    for k in Z_NEAR:
        z_copies[k].wait_recv()
    for copy in x_near.values():
        copy.start()

    def pass_on(r, onward=()):
        y_copies[r].wait_recv()
        for k in onward:
            y_copies[k].start()
        twins[r].start()

    pass_on(7)
    pass_on(1)
    pass_on(6, (5, 4))
    pass_on(2, (3, 8))
    for k in Z_FAR:
        z_copies[k].wait_recv()
    for copy in x_far.values():
        copy.start()

    def open_side(side):
        for r in Y_SIDES[side]:
            twins[r].wait_recv()
        total = jnp.zeros((1, 1), F32)
        span = slice(side * SIDE, (side + 1) * SIDE)
        rows_t[:, span] = jnp.transpose(rows[span, :])
        for r in range(side * NY, (side + 1) * NY):
            info = rows[r * RB + BOXP - 16 : r * RB + BOXP, :].astype(F32)
            flags = info[BOX - BOXP + 16 : BOX - BOXP + 17, 0:RB]
            limit[0:1, r * RB : (r + 1) * RB] = jnp.where(flags > 0.5, 100.0, -1000.0)
            count = info[BOX - BOXP + 17 : BOX - BOXP + 18, :]
            total = total + 16.0 * count[:, 0:1] + count[:, 1:2]
        return total

    bias_row = bias[...]
    logit_value = logit[0]

    seen, opened = set(), set()

    def open_group(r):
        value = toks[r].astype(F32).reshape(NZ, 2, OWN, HALF)
        value = jnp.concatenate([value[:, 0].reshape(GROUP, HALF), value[:, 1].reshape(GROUP, HALF)], axis=1)
        w[r] = value.astype(BF)
        wt[r // 2, :, r % 2 * GP : r % 2 * GP + GROUP] = jnp.transpose(value).astype(BF)
        column = (jnp.sum(value * bias_row, axis=1, keepdims=True) + logit_value) * LOG2E
        offset[r] = jnp.broadcast_to(column, (GROUP, HALF))

    def line(ref, missing):
        pad = jnp.full((1, BOXP - BOX), missing, jnp.int32)
        rest = jnp.full((1, D - RB), missing, jnp.int32)
        return jnp.concatenate([ref[0:1, :], pad, ref[1:2, :], pad, rest], axis=1)

    def slopes(r, side):
        span = slice(side * SIDE, (side + 1) * SIDE)
        raw = jnp.dot(w[r], rows_t[:, span], preferred_element_type=F32)
        score = jnp.minimum(raw * (LOG2E / 16.0) + offset[r][:, 0:1], limit[0:1, span])
        slope = negative_slope(score)
        if r == 0 and side == 0:
            start = line(begin, 1 << 20)
            stop = start + line(length, 0)
            index = iota((GROUP, D), 0)
            token_index = ((z + index // OWN + (NZ - SHIFT)) % NZ) * TOK + index % TOK
            image = (iota((GROUP, D), 1) >= BOXP).astype(jnp.int32)
            positive = (image == (index // TOK) % 2) & (token_index >= start) & (token_index < stop)
            positive = positive & (limit[0:1, 0:D] > 0.0)
            first = jnp.where(positive, positive_slope(score[:, 0:D]), slope[:, 0:D])
            slope = jnp.concatenate([first, slope[:, D:SIDE]], axis=1)
        total = slope[:, 0:HALF]
        for q in range(1, SIDE // HALF):
            total = total + slope[:, q * HALF : (q + 1) * HALF]
        csum[r] = total if r not in seen else csum[r] + total
        seen.add(r)
        g[side, r // 2, r % 2 * GP : r % 2 * GP + GROUP, :] = slope.astype(BF)

    def word_product(r, side):
        span = slice(side * SIDE, (side + 1) * SIDE)
        kept = g[side, r // 2, r % 2 * GP : r % 2 * GP + GROUP, :]
        grads = jnp.dot(kept, rows[span, :], preferred_element_type=F32)
        wp[r] = grads if r not in opened else wp[r] + grads
        opened.add(r)

    def region_product(pair, side, first):
        part = jnp.dot(wt[pair], g[side, pair], preferred_element_type=F32)
        rp[side] = part if first else rp[side] + part

    def close_group(r):
        column = jnp.sum(csum[r], axis=1, keepdims=True)
        return wp[r] + column * (16.0 * bias_row)

    rx_copies = {k: send(x_out.at[k - 1], x_in.at[k - 1], rx_send, rx_recv, k - 1, at_x(k)) for k in (1, 2, 3)}
    ry_copies = {
        r: send(y_out.at[k], y_in.at[k], ry_send, ry_recv, k, at_y(to))
        for k, (r, to) in enumerate(((1, 1), (7, 7), (3, 1), (5, 7), (2, 2), (6, 6)))
    }
    upper, lower = pl.ds(0, BOXP), pl.ds(BOXP, BOXP)
    ry_copies[4] = send(y_out.at[6, upper], y_in.at[6, upper], ry_send, ry_recv, 6, at_y(2))
    ry_copies[8] = send(y_out.at[6, lower], y_in.at[6, lower], ry_send, ry_recv, 7, at_y(6))
    twin_copies = {
        side: send(twin_out.at[side], twin_in.at[side], c_send, c_recv, NY + side, twin) for side in range(2)
    }
    n_x = {k: send(tally.at[0], tally_x.at[k - 1], n_send, n_recv, k - 1, at_x(k)) for k in (1, 3, 2)}
    n_z = {k: send(tally.at[1], tally_z.at[k - 1], n_send, n_recv, 2 + k, at_z(k)) for k in Z_ORDER}

    def words_of(r):
        x_near[NX - r].wait_recv()
        x_far[NX - r].wait_recv()
        open_group(r)

    def send_words(r):
        x_out[r - 1] = close_group(r).astype(BF)
        rx_copies[r].start()

    def other_core(side):
        twin_out[side] = jnp.transpose(rp[side][:, PART:SIDE]).astype(BF)
        twin_copies[side].start()

    def to_owners(side):
        twin_copies[side].wait_recv()
        both = jnp.transpose(rp[side][:, 0:PART]) + twin_in[side].astype(F32)
        kept = {0: 0, 2: 1, 6: 2}
        slots = {1: 0, 7: 1, 3: 2, 5: 3, 4: 6}
        for k, r in reversed(tuple(enumerate(Y_SIDES[side]))):
            part = both[k * RB : (k + 1) * RB, :]
            if r in kept:
                y_own[kept[r]] = part
            else:
                y_out[slots[r]] = part.astype(BF)
                ry_copies[r].start()
                if r == 4:
                    ry_copies[8].start()

    def pass_sums():
        for r, kept, near, far, part in ((2, 1, 3, 4, upper), (6, 2, 5, 8, lower)):
            slot, k = {2: 4, 6: 5}[r], {3: 2, 5: 3}[near]
            ry_copies[near].wait_recv()
            ry_copies[far].wait_recv()
            y_own[kept] = y_own[kept] + y_in[k].astype(F32)
            y_own[kept, part, :] = y_own[kept, part, :] + y_in[6, part, :].astype(F32)
            y_out[slot] = y_own[kept].astype(BF)
            ry_copies[r].start()

    open_group(0)
    counts = open_side(0)
    slopes(0, 0)
    word_product(0, 0)
    pass_on(5)
    pass_on(3)
    y_copies[8].wait_recv()
    pass_on(4)
    words_of(1)
    slopes(1, 0)
    word_product(1, 0)
    region_product(0, 0, True)
    words_of(2)
    words_of(3)
    counts = counts + open_side(1)
    tally[0] = jnp.broadcast_to(counts, (8, HALF))
    for copy in n_x.values():
        copy.start()

    slopes(2, 0)
    word_product(2, 0)
    slopes(2, 1)
    word_product(2, 1)
    send_words(2)
    slopes(3, 1)
    word_product(3, 1)
    region_product(1, 1, True)
    slopes(0, 1)
    word_product(0, 1)
    slopes(1, 1)
    region_product(0, 1, False)
    other_core(1)
    word_product(1, 1)
    send_words(1)
    for copy in n_x.values():
        copy.wait_recv()
    tally[1] = tally[0] + tally_x[0] + tally_x[1] + tally_x[2]
    for copy in n_z.values():
        copy.start()
    slopes(3, 0)
    word_product(3, 0)
    send_words(3)
    to_owners(1)
    region_product(1, 0, False)
    other_core(0)
    to_owners(0)

    sums = close_group(0)
    for k in (2, 1, 3):
        rx_copies[k].wait_recv()
        sums = sums + x_in[k - 1].astype(F32)
    sums = sums.reshape(NZ, OWN, D)
    halves = jnp.concatenate([sums[:, :, 0:HALF], sums[:, :, HALF:D]], axis=1)
    z_out[...] = halves.astype(BF)
    rz_copies = {
        k: send(z_out.at[(SHIFT + k) % NZ], z_in.at[k - 1], rz_send, rz_recv, k - 1, at_z(k)) for k in Z_ORDER
    }
    for k in reversed(Z_ORDER):
        rz_copies[k].start()
    chip = halves[SHIFT]
    pass_sums()

    positives = tally[1]
    for k in Z_ORDER:
        n_z[k].wait_recv()
        positives = positives + tally_z[k - 1]
    coef = (scale[0] * (1.5 / 16.0)) / positives[0:1, 0:1]

    for k in Z_ORDER:
        rz_copies[k].wait_recv()
        chip = chip + z_in[k - 1].astype(F32)
    value = jnp.concatenate([chip[0:OWN], chip[OWN:CB]], axis=1) * coef
    for cap in range(2):
        part = value[cap * TOK : (cap + 1) * TOK]
        word_out[cap] = jnp.where(TOK * z + tok < token[cap], part, 0.0).astype(BF)

    both = y_own[0]
    for k, r in ((0, 1), (1, 7), (4, 2), (5, 6)):
        ry_copies[r].wait_recv()
        both = both + y_in[k].astype(F32)
    for img in range(2):
        part = both[img * BOXP : (img + 1) * BOXP] * coef
        part = jnp.where(BOX * z + row < box[img], part, 0.0)
        region_out[img] = part[0:BOX].astype(BF)

    for copies in (z_copies, y_copies, twins, x_near, x_far, rx_copies, n_x, n_z, ry_copies, rz_copies, twin_copies):
        for copy in copies.values():
            copy.wait_send()


def on_device(
    regions,
    words,
    box_counts,
    token_counts,
    span_begin,
    span_length,
    bias_weight,
    logit_bias,
    loss_scale,
):
    vmem, in_hbm = pl.BlockSpec(memory_space=pltpu.VMEM), pl.BlockSpec(memory_space=pltpu.HBM)
    smem = pltpu.SMEM
    hold = pltpu.VMEM

    def sems(n):
        return [pltpu.SemaphoreType.DMA((n,))] * 2

    return pl.pallas_call(
        kernel,
        out_shape=(
            jax.ShapeDtypeStruct((2, BOX, D), BF),
            jax.ShapeDtypeStruct((2, TOK, D), BF),
        ),
        in_specs=[vmem] * 2 + [in_hbm] * 7,
        out_specs=(vmem, vmem),
        scratch_shapes=[
            smem((2,), jnp.int32),
            smem((2,), jnp.int32),
            smem((1,), F32),
            smem((1,), F32),
            hold((2, BOX), jnp.int32),
            hold((2, BOX), jnp.int32),
            hold((1, D), F32),
            hold((RB, D), F32),
            hold((ROWS, D), BF),
            hold((D, ROWS), BF),
            hold((8, ROWS), F32),
            hold((NX, NZ, CB, HALF), BF),
            hold((NX, GROUP, D), BF),
            hold((2, D, 2 * GP), BF),
            hold((NX, GROUP, HALF), F32),
            hold((2, 2, 2 * GP, SIDE), BF),
            hold((NX, GROUP, D), F32),
            hold((NX, GROUP, HALF), F32),
            hold((2, D, SIDE), F32),
            hold((2, PART, D), BF),
            hold((2, PART, D), BF),
            hold((NY - 1, RB, D), BF),
            hold((NY - 1, RB, D), BF),
            hold((3, RB, D), F32),
            hold((NX - 1, GROUP, D), BF),
            hold((NX - 1, GROUP, D), BF),
            hold((NZ, CB, HALF), BF),
            hold((NZ - 1, CB, HALF), BF),
            hold((2, 8, HALF), F32),
            hold((NX - 1, 8, HALF), F32),
            hold((NZ - 1, 8, HALF), F32),
            pltpu.SemaphoreType.DMA((7,)),
        ]
        + sems(NY) + sems(NZ - 1) + sems(6) + sems(NY + 2) + sems(NX + NZ - 2)
        + sems(NY) + sems(NX - 1) + sems(NZ - 1),
        compiler_params=pltpu.CompilerParams(
            collective_id=0, has_side_effects=True, vmem_limit_bytes=32 * 2**20
        ),
        name="alignment",
    )(
        regions, words, box_counts, token_counts, span_begin, span_length,
        bias_weight.reshape(1, D), logit_bias.reshape(1), loss_scale.reshape(1),
    )


def solution(mesh):
    in_specs = (
        P("dp", "text", None),
        P("dp", "text", None),
        P("dp"),
        P("dp"),
        P("dp", "text"),
        P("dp", "text"),
        P(),
        P(),
        P(),
    )
    out_specs = (P("dp", "text", None), P("dp", "text", None))
    return jax.shard_map(
        on_device, mesh=mesh, in_specs=in_specs, out_specs=out_specs, check_vma=False
    )
```

```python
import math

import jax
import jax.numpy as jnp
from jax import lax
from jax.experimental import pallas as pl
from jax.experimental.pallas import tpu as pltpu
from jax.sharding import PartitionSpec as P

MESH = pl.DeviceIdType.MESH
NX, NY, NZ = 4, 8, 12
D = 256
HALF = 128
BOX = 75
BOXP = 80
RB = 2 * BOXP
TOK = 12
OWN = 2 * TOK
CB = 2 * OWN
GROUP = NZ * OWN
NEAR = 7
SHIFT = 3
SIDE = NY * RB
ROWS = 2 * SIDE
BF = jnp.bfloat16
F32 = jnp.float32
LOG2E = math.log2(math.e)
Z_ORDER = (1, 11, 2, 10, 3, 9, 4, 8, 5, 7, 6)
Z_NEAR = Z_ORDER[:6]
Z_FAR = Z_ORDER[6:]
Y_SIDES = ((0, 1, 7, 2), (6, 5, 3, 4))
GP = 384
PART = len(Y_SIDES[0]) * RB


def iota(shape, dim):
    return lax.broadcasted_iota(jnp.int32, shape, dim)


def negative_slope(score):
    grown = jnp.exp2(score)
    total = 1.0 + grown
    rest = 1.0 / total
    prob = grown * rest
    lost = jnp.log(total) + (grown - (total - 1.0))
    return prob * prob * (0.5 * prob + rest * lost)


def positive_slope(score):
    small = jnp.exp2(-jnp.abs(score))
    total = 1.0 + small
    part = 1.0 / total
    prob = jnp.where(score >= 0.0, part, small * part)
    rest = jnp.where(score >= 0.0, small * part, part)
    lost = jnp.log(total) + (small - (total - 1.0)) + jnp.maximum(-score, 0.0) * math.log(2.0)
    return (-1.0 / 6.0) * rest * rest * (2.0 * prob * lost + rest)


def kernel(
    regions, words, box_hbm, token_hbm, begin_hbm, length_hbm, bias_hbm, logit_hbm, scale_hbm,
    region_out, word_out,
    box, token, logit, scale, begin, length, bias,
    wide, rows, rows_t, limit, toks, w, wt, offset, g, wp, csum, rp,
    twin_out, twin_in, y_out, y_in, y_own, x_out, x_in, z_out, z_in,
    tally, tally_x, tally_z,
    l_sem, y_send, y_recv, z_send, z_recv, x_send, x_recv, c_send, c_recv, n_send, n_recv,
    ry_send, ry_recv, rx_send, rx_recv, rz_send, rz_recv,
):
    dp = lax.axis_index("dp")
    z = lax.axis_index("text")
    x, y, c = dp // (NY * 2), (dp // 2) % NY, dp % 2

    def at_x(k):
        return (((x + k) % NX) * NY + y) * 2 + c, z

    def at_y(k):
        return (x * NY + (y + k) % NY) * 2 + c, z

    def at_z(k):
        return dp, (z + k) % NZ

    twin = ((x * NY + y) * 2 + 1 - c, z)

    def send(src, dst, sends, recvs, k, dev):
        return pltpu.make_async_remote_copy(
            src_ref=src, dst_ref=dst, send_sem=sends.at[k], recv_sem=recvs.at[k], device_id=dev, device_id_type=MESH
        )

    barrier = pltpu.get_barrier_semaphore()
    peers = [at_z(k) for k in Z_ORDER] + [at_y(k) for k in (1, 7, 2, 6)] + [at_x(k) for k in (1, 3, 2)] + [twin]
    for dev in peers:
        pl.semaphore_signal(barrier, inc=1, device_id=dev, device_id_type=MESH)
    staged = (
        (box_hbm, box), (token_hbm, token), (begin_hbm, begin), (length_hbm, length), (bias_hbm, bias),
        (logit_hbm, logit), (scale_hbm, scale),
    )
    loads = [pltpu.make_async_copy(src, dst, l_sem.at[k]) for k, (src, dst) in enumerate(staged)]
    for load in loads:
        load.start()
    for load in loads:
        load.wait()

    tok = iota((TOK, D), 0)
    for cap in range(2):
        value = words[cap].astype(F32)
        wide[cap * TOK : (cap + 1) * TOK, :] = jnp.where(TOK * z + tok < token[cap], value, 0.0)
    mine = wide[0:OWN, :]
    toks[0, SHIFT] = jnp.concatenate([mine[:, 0:HALF], mine[:, HALF:D]], axis=0).astype(BF)

    count = jnp.zeros((1, 1), F32)
    for img in range(2):
        valid = BOX * z + iota((1, BOX), 1) < box[img]
        count = count + jnp.sum(jnp.where(valid, length[img : img + 1, :], 0).astype(F32), axis=1, keepdims=True)
    high = jnp.floor(count * (1.0 / 16.0))
    low = count - 16.0 * high
    lane, row = iota((BOXP, D), 1), iota((BOXP, D), 0)
    slot = jnp.where(lane < BOXP, lane, lane - BOXP)
    flag = (slot < BOX) & (lane < RB) & (BOX * z + slot < jnp.where(lane < BOXP, box[0], box[1]))
    for img in range(2):
        wide[img * BOXP + BOXP - 8 : (img + 1) * BOXP, :] = jnp.zeros((8, D), F32)
        wide[img * BOXP : img * BOXP + BOX, :] = regions[img].astype(F32)
        value = wide[img * BOXP : (img + 1) * BOXP, :]
        value = jnp.where((row < BOX) & (BOX * z + row < box[img]), value, 0.0)
        if img == 0:
            value = jnp.where((row == BOX) & flag, 1.0, value)
            value = jnp.where((row == BOX + 1) & (lane == 0), high, value)
            value = jnp.where((row == BOX + 1) & (lane == 1), low, value)
        rows[img * BOXP : (img + 1) * BOXP, :] = value.astype(BF)

    wt[...] = jnp.zeros_like(wt)
    for side in range(2):
        for r in range(NX):
            g[side, r // 2, r % 2 * GP + GROUP : (r % 2 + 1) * GP, :] = jnp.zeros((GP - GROUP, SIDE), BF)
    pl.semaphore_wait(barrier, len(peers))

    def where(r, other):
        side = 0 if r in Y_SIDES[0] else 1
        return (side * 2 + other) * PART + Y_SIDES[side].index(r) * RB

    def block(r, other=0):
        return rows.at[pl.ds(where(r, other), RB)]

    z_copies = {
        k: send(toks.at[0, SHIFT], toks.at[0, (SHIFT - k) % NZ], z_send, z_recv, k - 1, at_z(k)) for k in Z_ORDER
    }
    def half(r, k):
        return rows.at[pl.ds(where(r, 0) + k * BOXP, BOXP)]

    y_copies = {
        r: send(block(0), block(r), y_send, y_recv, k, at_y(NY - r)) for k, r in enumerate((7, 1, 6, 2))
    }
    y_copies[5] = send(block(6), block(5), y_send, y_recv, 4, at_y(1))
    y_copies[3] = send(block(2), block(3), y_send, y_recv, 5, at_y(7))
    y_copies[4] = send(half(6, 0), half(4, 0), y_send, y_recv, 6, at_y(2))
    y_copies[8] = send(half(2, 1), half(4, 1), y_send, y_recv, 7, at_y(6))
    twins = {r: send(block(r), block(r, 1), c_send, c_recv, r, twin) for r in range(NY)}
    near, far = pl.ds(0, NEAR), pl.ds(NEAR, NZ - NEAR)
    x_near = {k: send(toks.at[0, near], toks.at[NX - k, near], x_send, x_recv, k - 1, at_x(k)) for k in (2, 1, 3)}
    x_far = {k: send(toks.at[0, far], toks.at[NX - k, far], x_send, x_recv, 2 + k, at_x(k)) for k in (2, 1, 3)}
    for k in Z_ORDER:
        z_copies[k].start()
    for r in (7, 1, 6, 2):
        y_copies[r].start()
    twins[0].start()
    for k in Z_NEAR:
        z_copies[k].wait_recv()
    for copy in x_near.values():
        copy.start()

    def pass_on(r, onward=()):
        y_copies[r].wait_recv()
        for k in onward:
            y_copies[k].start()
        twins[r].start()

    pass_on(7)
    pass_on(1)
    pass_on(6, (5, 4))
    pass_on(2, (3, 8))
    for k in Z_FAR:
        z_copies[k].wait_recv()
    for copy in x_far.values():
        copy.start()

    def open_side(side):
        for r in Y_SIDES[side]:
            twins[r].wait_recv()
        total = jnp.zeros((1, 1), F32)
        span = slice(side * SIDE, (side + 1) * SIDE)
        rows_t[:, span] = jnp.transpose(rows[span, :])
        for r in range(side * NY, (side + 1) * NY):
            info = rows[r * RB + BOXP - 16 : r * RB + BOXP, :].astype(F32)
            flags = info[BOX - BOXP + 16 : BOX - BOXP + 17, 0:RB]
            limit[0:1, r * RB : (r + 1) * RB] = jnp.where(flags > 0.5, 100.0, -1000.0)
            count = info[BOX - BOXP + 17 : BOX - BOXP + 18, :]
            total = total + 16.0 * count[:, 0:1] + count[:, 1:2]
        return total

    bias_row = bias[...]
    logit_value = logit[0]

    seen, opened = set(), set()

    def open_group(r):
        value = toks[r].astype(F32).reshape(NZ, 2, OWN, HALF)
        value = jnp.concatenate([value[:, 0].reshape(GROUP, HALF), value[:, 1].reshape(GROUP, HALF)], axis=1)
        w[r] = value.astype(BF)
        wt[r // 2, :, r % 2 * GP : r % 2 * GP + GROUP] = jnp.transpose(value).astype(BF)
        column = (jnp.sum(value * bias_row, axis=1, keepdims=True) + logit_value) * LOG2E
        offset[r] = jnp.broadcast_to(column, (GROUP, HALF))

    def line(ref, missing):
        pad = jnp.full((1, BOXP - BOX), missing, jnp.int32)
        rest = jnp.full((1, D - RB), missing, jnp.int32)
        return jnp.concatenate([ref[0:1, :], pad, ref[1:2, :], pad, rest], axis=1)

    def slopes(r, side):
        span = slice(side * SIDE, (side + 1) * SIDE)
        raw = jnp.dot(w[r], rows_t[:, span], preferred_element_type=F32)
        score = jnp.minimum(raw * (LOG2E / 16.0) + offset[r][:, 0:1], limit[0:1, span])
        slope = negative_slope(score)
        if r == 0 and side == 0:
            start = line(begin, 1 << 20)
            stop = start + line(length, 0)
            index = iota((GROUP, D), 0)
            token_index = ((z + index // OWN + (NZ - SHIFT)) % NZ) * TOK + index % TOK
            image = (iota((GROUP, D), 1) >= BOXP).astype(jnp.int32)
            positive = (image == (index // TOK) % 2) & (token_index >= start) & (token_index < stop)
            positive = positive & (limit[0:1, 0:D] > 0.0)
            first = jnp.where(positive, positive_slope(score[:, 0:D]), slope[:, 0:D])
            slope = jnp.concatenate([first, slope[:, D:SIDE]], axis=1)
        total = slope[:, 0:HALF]
        for q in range(1, SIDE // HALF):
            total = total + slope[:, q * HALF : (q + 1) * HALF]
        csum[r] = total if r not in seen else csum[r] + total
        seen.add(r)
        g[side, r // 2, r % 2 * GP : r % 2 * GP + GROUP, :] = slope.astype(BF)

    def word_product(r, side):
        span = slice(side * SIDE, (side + 1) * SIDE)
        kept = g[side, r // 2, r % 2 * GP : r % 2 * GP + GROUP, :]
        grads = jnp.dot(kept, rows[span, :], preferred_element_type=F32)
        wp[r] = grads if r not in opened else wp[r] + grads
        opened.add(r)

    def region_product(pair, side, first):
        part = jnp.dot(wt[pair], g[side, pair], preferred_element_type=F32)
        rp[side] = part if first else rp[side] + part

    def close_group(r):
        column = jnp.sum(csum[r], axis=1, keepdims=True)
        return wp[r] + column * (16.0 * bias_row)

    rx_copies = {k: send(x_out.at[k - 1], x_in.at[k - 1], rx_send, rx_recv, k - 1, at_x(k)) for k in (1, 2, 3)}
    ry_copies = {
        r: send(y_out.at[k], y_in.at[k], ry_send, ry_recv, k, at_y(to))
        for k, (r, to) in enumerate(((1, 1), (7, 7), (3, 1), (5, 7), (2, 2), (6, 6)))
    }
    upper, lower = pl.ds(0, BOXP), pl.ds(BOXP, BOXP)
    ry_copies[4] = send(y_out.at[6, upper], y_in.at[6, upper], ry_send, ry_recv, 6, at_y(2))
    ry_copies[8] = send(y_out.at[6, lower], y_in.at[6, lower], ry_send, ry_recv, 7, at_y(6))
    twin_copies = {
        side: send(twin_out.at[side], twin_in.at[side], c_send, c_recv, NY + side, twin) for side in range(2)
    }
    n_x = {k: send(tally.at[0], tally_x.at[k - 1], n_send, n_recv, k - 1, at_x(k)) for k in (1, 3, 2)}
    n_z = {k: send(tally.at[1], tally_z.at[k - 1], n_send, n_recv, 2 + k, at_z(k)) for k in Z_ORDER}

    def words_of(r):
        x_near[NX - r].wait_recv()
        x_far[NX - r].wait_recv()
        open_group(r)

    def send_words(r):
        x_out[r - 1] = close_group(r).astype(BF)
        rx_copies[r].start()

    def other_core(side):
        twin_out[side] = jnp.transpose(rp[side][:, PART:SIDE]).astype(BF)
        twin_copies[side].start()

    def to_owners(side):
        twin_copies[side].wait_recv()
        both = jnp.transpose(rp[side][:, 0:PART]) + twin_in[side].astype(F32)
        kept = {0: 0, 2: 1, 6: 2}
        slots = {1: 0, 7: 1, 3: 2, 5: 3, 4: 6}
        for k, r in reversed(tuple(enumerate(Y_SIDES[side]))):
            part = both[k * RB : (k + 1) * RB, :]
            if r in kept:
                y_own[kept[r]] = part
            else:
                y_out[slots[r]] = part.astype(BF)
                ry_copies[r].start()
                if r == 4:
                    ry_copies[8].start()

    def pass_sums():
        for r, kept, near, far, part in ((2, 1, 3, 4, upper), (6, 2, 5, 8, lower)):
            slot, k = {2: 4, 6: 5}[r], {3: 2, 5: 3}[near]
            ry_copies[near].wait_recv()
            ry_copies[far].wait_recv()
            y_own[kept] = y_own[kept] + y_in[k].astype(F32)
            y_own[kept, part, :] = y_own[kept, part, :] + y_in[6, part, :].astype(F32)
            y_out[slot] = y_own[kept].astype(BF)
            ry_copies[r].start()

    open_group(0)
    counts = open_side(0)
    slopes(0, 0)
    word_product(0, 0)
    pass_on(5)
    pass_on(3)
    y_copies[8].wait_recv()
    pass_on(4)
    words_of(1)
    slopes(1, 0)
    word_product(1, 0)
    region_product(0, 0, True)
    words_of(2)

    slopes(2, 0)
    word_product(2, 0)
    words_of(3)
    counts = counts + open_side(1)
    tally[0] = jnp.broadcast_to(counts, (8, HALF))
    for copy in n_x.values():
        copy.start()
    slopes(2, 1)
    word_product(2, 1)
    send_words(2)
    slopes(3, 1)
    word_product(3, 1)
    region_product(1, 1, True)
    slopes(0, 1)
    word_product(0, 1)
    slopes(1, 1)
    region_product(0, 1, False)
    other_core(1)
    word_product(1, 1)
    send_words(1)
    for copy in n_x.values():
        copy.wait_recv()
    tally[1] = tally[0] + tally_x[0] + tally_x[1] + tally_x[2]
    for copy in n_z.values():
        copy.start()
    slopes(3, 0)
    word_product(3, 0)
    send_words(3)
    to_owners(1)
    region_product(1, 0, False)
    other_core(0)
    to_owners(0)

    sums = close_group(0)
    for k in (2, 1, 3):
        rx_copies[k].wait_recv()
        sums = sums + x_in[k - 1].astype(F32)
    sums = sums.reshape(NZ, OWN, D)
    halves = jnp.concatenate([sums[:, :, 0:HALF], sums[:, :, HALF:D]], axis=1)
    z_out[...] = halves.astype(BF)
    rz_copies = {
        k: send(z_out.at[(SHIFT + k) % NZ], z_in.at[k - 1], rz_send, rz_recv, k - 1, at_z(k)) for k in Z_ORDER
    }
    for k in reversed(Z_ORDER):
        rz_copies[k].start()
    chip = halves[SHIFT]
    pass_sums()

    positives = tally[1]
    for k in Z_ORDER:
        n_z[k].wait_recv()
        positives = positives + tally_z[k - 1]
    coef = (scale[0] * (1.5 / 16.0)) / positives[0:1, 0:1]

    for k in Z_ORDER:
        rz_copies[k].wait_recv()
        chip = chip + z_in[k - 1].astype(F32)
    value = jnp.concatenate([chip[0:OWN], chip[OWN:CB]], axis=1) * coef
    for cap in range(2):
        part = value[cap * TOK : (cap + 1) * TOK]
        word_out[cap] = jnp.where(TOK * z + tok < token[cap], part, 0.0).astype(BF)

    both = y_own[0]
    for k, r in ((0, 1), (1, 7), (4, 2), (5, 6)):
        ry_copies[r].wait_recv()
        both = both + y_in[k].astype(F32)
    for img in range(2):
        part = both[img * BOXP : (img + 1) * BOXP] * coef
        part = jnp.where(BOX * z + row < box[img], part, 0.0)
        region_out[img] = part[0:BOX].astype(BF)

    for copies in (z_copies, y_copies, twins, x_near, x_far, rx_copies, n_x, n_z, ry_copies, rz_copies, twin_copies):
        for copy in copies.values():
            copy.wait_send()


def on_device(
    regions,
    words,
    box_counts,
    token_counts,
    span_begin,
    span_length,
    bias_weight,
    logit_bias,
    loss_scale,
):
    vmem, in_hbm = pl.BlockSpec(memory_space=pltpu.VMEM), pl.BlockSpec(memory_space=pltpu.HBM)
    smem = pltpu.SMEM
    hold = pltpu.VMEM

    def sems(n):
        return [pltpu.SemaphoreType.DMA((n,))] * 2

    return pl.pallas_call(
        kernel,
        out_shape=(
            jax.ShapeDtypeStruct((2, BOX, D), BF),
            jax.ShapeDtypeStruct((2, TOK, D), BF),
        ),
        in_specs=[vmem] * 2 + [in_hbm] * 7,
        out_specs=(vmem, vmem),
        scratch_shapes=[
            smem((2,), jnp.int32),
            smem((2,), jnp.int32),
            smem((1,), F32),
            smem((1,), F32),
            hold((2, BOX), jnp.int32),
            hold((2, BOX), jnp.int32),
            hold((1, D), F32),
            hold((RB, D), F32),
            hold((ROWS, D), BF),
            hold((D, ROWS), BF),
            hold((8, ROWS), F32),
            hold((NX, NZ, CB, HALF), BF),
            hold((NX, GROUP, D), BF),
            hold((2, D, 2 * GP), BF),
            hold((NX, GROUP, HALF), F32),
            hold((2, 2, 2 * GP, SIDE), BF),
            hold((NX, GROUP, D), F32),
            hold((NX, GROUP, HALF), F32),
            hold((2, D, SIDE), F32),
            hold((2, PART, D), BF),
            hold((2, PART, D), BF),
            hold((NY - 1, RB, D), BF),
            hold((NY - 1, RB, D), BF),
            hold((3, RB, D), F32),
            hold((NX - 1, GROUP, D), BF),
            hold((NX - 1, GROUP, D), BF),
            hold((NZ, CB, HALF), BF),
            hold((NZ - 1, CB, HALF), BF),
            hold((2, 8, HALF), F32),
            hold((NX - 1, 8, HALF), F32),
            hold((NZ - 1, 8, HALF), F32),
            pltpu.SemaphoreType.DMA((7,)),
        ]
        + sems(NY) + sems(NZ - 1) + sems(6) + sems(NY + 2) + sems(NX + NZ - 2)
        + sems(NY) + sems(NX - 1) + sems(NZ - 1),
        compiler_params=pltpu.CompilerParams(
            collective_id=0, has_side_effects=True, vmem_limit_bytes=32 * 2**20
        ),
        name="alignment",
    )(
        regions, words, box_counts, token_counts, span_begin, span_length,
        bias_weight.reshape(1, D), logit_bias.reshape(1), loss_scale.reshape(1),
    )


def solution(mesh):
    in_specs = (
        P("dp", "text", None),
        P("dp", "text", None),
        P("dp"),
        P("dp"),
        P("dp", "text"),
        P("dp", "text"),
        P(),
        P(),
        P(),
    )
    out_specs = (P("dp", "text", None), P("dp", "text", None))
    return jax.shard_map(
        on_device, mesh=mesh, in_specs=in_specs, out_specs=out_specs, check_vma=False
    )
```

```python
import math

import jax
import jax.numpy as jnp
from jax import lax
from jax.experimental import pallas as pl
from jax.experimental.pallas import tpu as pltpu
from jax.sharding import PartitionSpec as P

MESH = pl.DeviceIdType.MESH
NX, NY, NZ = 4, 8, 12
D = 256
HALF = 128
BOX = 75
BOXP = 80
RB = 2 * BOXP
TOK = 12
OWN = 2 * TOK
CB = 2 * OWN
GROUP = NZ * OWN
NEAR = 7
SHIFT = 3
SIDE = NY * RB
ROWS = 2 * SIDE
BF = jnp.bfloat16
F32 = jnp.float32
LOG2E = math.log2(math.e)
Z_ORDER = (1, 11, 2, 10, 3, 9, 4, 8, 5, 7, 6)
Z_NEAR = Z_ORDER[:6]
Z_FAR = Z_ORDER[6:]
Y_SIDES = ((0, 1, 7, 2), (6, 5, 3, 4))
GP = 384
PART = len(Y_SIDES[0]) * RB


def iota(shape, dim):
    return lax.broadcasted_iota(jnp.int32, shape, dim)


def negative_slope(score):
    grown = jnp.exp2(score)
    total = 1.0 + grown
    rest = 1.0 / total
    prob = grown * rest
    lost = jnp.log(total) + (1.5 * grown - (total - 1.0))
    return prob * prob * rest * lost


def positive_slope(score):
    small = jnp.exp2(-jnp.abs(score))
    total = 1.0 + small
    part = 1.0 / total
    prob = jnp.where(score >= 0.0, part, small * part)
    rest = jnp.where(score >= 0.0, small * part, part)
    lost = jnp.log(total) + (small - (total - 1.0)) + jnp.maximum(-score, 0.0) * math.log(2.0)
    return (-1.0 / 6.0) * rest * rest * (2.0 * prob * lost + rest)


def kernel(
    regions, words, box_hbm, token_hbm, begin_hbm, length_hbm, bias_hbm, logit_hbm, scale_hbm,
    region_out, word_out,
    box, token, logit, scale, begin, length, bias,
    wide, rows, rows_t, limit, toks, w, wt, offset, g, wp, csum, rp,
    twin_out, twin_in, y_out, y_in, y_own, x_out, x_in, z_out, z_in,
    tally, tally_x, tally_z,
    l_sem, y_send, y_recv, z_send, z_recv, x_send, x_recv, c_send, c_recv, n_send, n_recv,
    ry_send, ry_recv, rx_send, rx_recv, rz_send, rz_recv,
):
    dp = lax.axis_index("dp")
    z = lax.axis_index("text")
    x, y, c = dp // (NY * 2), (dp // 2) % NY, dp % 2

    def at_x(k):
        return (((x + k) % NX) * NY + y) * 2 + c, z

    def at_y(k):
        return (x * NY + (y + k) % NY) * 2 + c, z

    def at_z(k):
        return dp, (z + k) % NZ

    twin = ((x * NY + y) * 2 + 1 - c, z)

    def send(src, dst, sends, recvs, k, dev):
        return pltpu.make_async_remote_copy(
            src_ref=src, dst_ref=dst, send_sem=sends.at[k], recv_sem=recvs.at[k], device_id=dev, device_id_type=MESH
        )

    barrier = pltpu.get_barrier_semaphore()
    peers = [at_z(k) for k in Z_ORDER] + [at_y(k) for k in (1, 7, 2, 6)] + [at_x(k) for k in (1, 3, 2)] + [twin]
    for dev in peers:
        pl.semaphore_signal(barrier, inc=1, device_id=dev, device_id_type=MESH)
    staged = (
        (box_hbm, box), (token_hbm, token), (begin_hbm, begin), (length_hbm, length), (bias_hbm, bias),
        (logit_hbm, logit), (scale_hbm, scale),
    )
    loads = [pltpu.make_async_copy(src, dst, l_sem.at[k]) for k, (src, dst) in enumerate(staged)]
    for load in loads:
        load.start()
    for load in loads:
        load.wait()

    tok = iota((TOK, D), 0)
    for cap in range(2):
        value = words[cap].astype(F32)
        wide[cap * TOK : (cap + 1) * TOK, :] = jnp.where(TOK * z + tok < token[cap], value, 0.0)
    mine = wide[0:OWN, :]
    toks[0, SHIFT] = jnp.concatenate([mine[:, 0:HALF], mine[:, HALF:D]], axis=0).astype(BF)

    count = jnp.zeros((1, 1), F32)
    for img in range(2):
        valid = BOX * z + iota((1, BOX), 1) < box[img]
        count = count + jnp.sum(jnp.where(valid, length[img : img + 1, :], 0).astype(F32), axis=1, keepdims=True)
    high = jnp.floor(count * (1.0 / 16.0))
    low = count - 16.0 * high
    lane, row = iota((BOXP, D), 1), iota((BOXP, D), 0)
    slot = jnp.where(lane < BOXP, lane, lane - BOXP)
    flag = (slot < BOX) & (lane < RB) & (BOX * z + slot < jnp.where(lane < BOXP, box[0], box[1]))
    for img in range(2):
        wide[img * BOXP + BOXP - 8 : (img + 1) * BOXP, :] = jnp.zeros((8, D), F32)
        wide[img * BOXP : img * BOXP + BOX, :] = regions[img].astype(F32)
        value = wide[img * BOXP : (img + 1) * BOXP, :]
        value = jnp.where((row < BOX) & (BOX * z + row < box[img]), value, 0.0)
        if img == 0:
            value = jnp.where((row == BOX) & flag, 1.0, value)
            value = jnp.where((row == BOX + 1) & (lane == 0), high, value)
            value = jnp.where((row == BOX + 1) & (lane == 1), low, value)
        rows[img * BOXP : (img + 1) * BOXP, :] = value.astype(BF)

    wt[...] = jnp.zeros_like(wt)
    for side in range(2):
        for r in range(NX):
            g[side, r // 2, r % 2 * GP + GROUP : (r % 2 + 1) * GP, :] = jnp.zeros((GP - GROUP, SIDE), BF)
    pl.semaphore_wait(barrier, len(peers))

    def where(r, other):
        side = 0 if r in Y_SIDES[0] else 1
        return (side * 2 + other) * PART + Y_SIDES[side].index(r) * RB

    def block(r, other=0):
        return rows.at[pl.ds(where(r, other), RB)]

    z_copies = {
        k: send(toks.at[0, SHIFT], toks.at[0, (SHIFT - k) % NZ], z_send, z_recv, k - 1, at_z(k)) for k in Z_ORDER
    }
    def half(r, k):
        return rows.at[pl.ds(where(r, 0) + k * BOXP, BOXP)]

    y_copies = {
        r: send(block(0), block(r), y_send, y_recv, k, at_y(NY - r)) for k, r in enumerate((7, 1, 6, 2))
    }
    y_copies[5] = send(block(6), block(5), y_send, y_recv, 4, at_y(1))
    y_copies[3] = send(block(2), block(3), y_send, y_recv, 5, at_y(7))
    y_copies[4] = send(half(6, 0), half(4, 0), y_send, y_recv, 6, at_y(2))
    y_copies[8] = send(half(2, 1), half(4, 1), y_send, y_recv, 7, at_y(6))
    twins = {r: send(block(r), block(r, 1), c_send, c_recv, r, twin) for r in range(NY)}
    near, far = pl.ds(0, NEAR), pl.ds(NEAR, NZ - NEAR)
    x_near = {k: send(toks.at[0, near], toks.at[NX - k, near], x_send, x_recv, k - 1, at_x(k)) for k in (2, 1, 3)}
    x_far = {k: send(toks.at[0, far], toks.at[NX - k, far], x_send, x_recv, 2 + k, at_x(k)) for k in (2, 1, 3)}
    for k in Z_ORDER:
        z_copies[k].start()
    for r in (7, 1, 6, 2):
        y_copies[r].start()
    twins[0].start()
    for k in Z_NEAR:
        z_copies[k].wait_recv()
    for copy in x_near.values():
        copy.start()

    def pass_on(r, onward=()):
        y_copies[r].wait_recv()
        for k in onward:
            y_copies[k].start()
        twins[r].start()

    pass_on(7)
    pass_on(1)
    pass_on(6, (5, 4))
    pass_on(2, (3, 8))
    for k in Z_FAR:
        z_copies[k].wait_recv()
    for copy in x_far.values():
        copy.start()

    def open_side(side):
        for r in Y_SIDES[side]:
            twins[r].wait_recv()
        total = jnp.zeros((1, 1), F32)
        span = slice(side * SIDE, (side + 1) * SIDE)
        rows_t[:, span] = jnp.transpose(rows[span, :])
        for r in range(side * NY, (side + 1) * NY):
            info = rows[r * RB + BOXP - 16 : r * RB + BOXP, :].astype(F32)
            flags = info[BOX - BOXP + 16 : BOX - BOXP + 17, 0:RB]
            limit[0:1, r * RB : (r + 1) * RB] = jnp.where(flags > 0.5, 100.0, -1000.0)
            count = info[BOX - BOXP + 17 : BOX - BOXP + 18, :]
            total = total + 16.0 * count[:, 0:1] + count[:, 1:2]
        return total

    bias_row = bias[...]
    logit_value = logit[0]

    seen, opened = set(), set()

    def open_group(r):
        value = toks[r].astype(F32).reshape(NZ, 2, OWN, HALF)
        value = jnp.concatenate([value[:, 0].reshape(GROUP, HALF), value[:, 1].reshape(GROUP, HALF)], axis=1)
        w[r] = value.astype(BF)
        wt[r // 2, :, r % 2 * GP : r % 2 * GP + GROUP] = jnp.transpose(value).astype(BF)
        column = (jnp.sum(value * bias_row, axis=1, keepdims=True) + logit_value) * LOG2E
        offset[r] = jnp.broadcast_to(column, (GROUP, HALF))

    def line(ref, missing):
        pad = jnp.full((1, BOXP - BOX), missing, jnp.int32)
        rest = jnp.full((1, D - RB), missing, jnp.int32)
        return jnp.concatenate([ref[0:1, :], pad, ref[1:2, :], pad, rest], axis=1)

    def slopes(r, side):
        span = slice(side * SIDE, (side + 1) * SIDE)
        raw = jnp.dot(w[r], rows_t[:, span], preferred_element_type=F32)
        score = jnp.minimum(raw * (LOG2E / 16.0) + offset[r][:, 0:1], limit[0:1, span])
        slope = negative_slope(score)
        if r == 0 and side == 0:
            start = line(begin, 1 << 20)
            stop = start + line(length, 0)
            index = iota((GROUP, D), 0)
            token_index = ((z + index // OWN + (NZ - SHIFT)) % NZ) * TOK + index % TOK
            image = (iota((GROUP, D), 1) >= BOXP).astype(jnp.int32)
            positive = (image == (index // TOK) % 2) & (token_index >= start) & (token_index < stop)
            positive = positive & (limit[0:1, 0:D] > 0.0)
            first = jnp.where(positive, positive_slope(score[:, 0:D]), slope[:, 0:D])
            slope = jnp.concatenate([first, slope[:, D:SIDE]], axis=1)
        total = slope[:, 0:HALF]
        for q in range(1, SIDE // HALF):
            total = total + slope[:, q * HALF : (q + 1) * HALF]
        csum[r] = total if r not in seen else csum[r] + total
        seen.add(r)
        g[side, r // 2, r % 2 * GP : r % 2 * GP + GROUP, :] = slope.astype(BF)

    def word_product(r, side):
        span = slice(side * SIDE, (side + 1) * SIDE)
        kept = g[side, r // 2, r % 2 * GP : r % 2 * GP + GROUP, :]
        grads = jnp.dot(kept, rows[span, :], preferred_element_type=F32)
        wp[r] = grads if r not in opened else wp[r] + grads
        opened.add(r)

    def region_product(pair, side, first):
        part = jnp.dot(wt[pair], g[side, pair], preferred_element_type=F32)
        rp[side] = part if first else rp[side] + part

    def close_group(r):
        column = jnp.sum(csum[r], axis=1, keepdims=True)
        return wp[r] + column * (16.0 * bias_row)

    rx_copies = {k: send(x_out.at[k - 1], x_in.at[k - 1], rx_send, rx_recv, k - 1, at_x(k)) for k in (1, 2, 3)}
    ry_copies = {
        r: send(y_out.at[k], y_in.at[k], ry_send, ry_recv, k, at_y(to))
        for k, (r, to) in enumerate(((1, 1), (7, 7), (3, 1), (5, 7), (2, 2), (6, 6)))
    }
    upper, lower = pl.ds(0, BOXP), pl.ds(BOXP, BOXP)
    ry_copies[4] = send(y_out.at[6, upper], y_in.at[6, upper], ry_send, ry_recv, 6, at_y(2))
    ry_copies[8] = send(y_out.at[6, lower], y_in.at[6, lower], ry_send, ry_recv, 7, at_y(6))
    twin_copies = {
        side: send(twin_out.at[side], twin_in.at[side], c_send, c_recv, NY + side, twin) for side in range(2)
    }
    n_x = {k: send(tally.at[0], tally_x.at[k - 1], n_send, n_recv, k - 1, at_x(k)) for k in (1, 3, 2)}
    n_z = {k: send(tally.at[1], tally_z.at[k - 1], n_send, n_recv, 2 + k, at_z(k)) for k in Z_ORDER}

    def words_of(r):
        x_near[NX - r].wait_recv()
        x_far[NX - r].wait_recv()
        open_group(r)

    def send_words(r):
        x_out[r - 1] = close_group(r).astype(BF)
        rx_copies[r].start()

    def other_core(side):
        twin_out[side] = jnp.transpose(rp[side][:, PART:SIDE]).astype(BF)
        twin_copies[side].start()

    def to_owners(side):
        twin_copies[side].wait_recv()
        both = jnp.transpose(rp[side][:, 0:PART]) + twin_in[side].astype(F32)
        kept = {0: 0, 2: 1, 6: 2}
        slots = {1: 0, 7: 1, 3: 2, 5: 3, 4: 6}
        for k, r in reversed(tuple(enumerate(Y_SIDES[side]))):
            part = both[k * RB : (k + 1) * RB, :]
            if r in kept:
                y_own[kept[r]] = part
            else:
                y_out[slots[r]] = part.astype(BF)
                ry_copies[r].start()
                if r == 4:
                    ry_copies[8].start()

    def pass_sums():
        for r, kept, near, far, part in ((2, 1, 3, 4, upper), (6, 2, 5, 8, lower)):
            slot, k = {2: 4, 6: 5}[r], {3: 2, 5: 3}[near]
            ry_copies[near].wait_recv()
            ry_copies[far].wait_recv()
            y_own[kept] = y_own[kept] + y_in[k].astype(F32)
            y_own[kept, part, :] = y_own[kept, part, :] + y_in[6, part, :].astype(F32)
            y_out[slot] = y_own[kept].astype(BF)
            ry_copies[r].start()

    open_group(0)
    counts = open_side(0)
    slopes(0, 0)
    word_product(0, 0)
    pass_on(5)
    pass_on(3)
    y_copies[8].wait_recv()
    pass_on(4)
    words_of(1)
    slopes(1, 0)
    word_product(1, 0)
    region_product(0, 0, True)
    words_of(2)

    slopes(2, 0)
    word_product(2, 0)
    words_of(3)
    counts = counts + open_side(1)
    tally[0] = jnp.broadcast_to(counts, (8, HALF))
    for copy in n_x.values():
        copy.start()
    slopes(2, 1)
    word_product(2, 1)
    send_words(2)
    slopes(3, 1)
    word_product(3, 1)
    region_product(1, 1, True)
    slopes(0, 1)
    word_product(0, 1)
    slopes(1, 1)
    region_product(0, 1, False)
    other_core(1)
    word_product(1, 1)
    send_words(1)
    for copy in n_x.values():
        copy.wait_recv()
    tally[1] = tally[0] + tally_x[0] + tally_x[1] + tally_x[2]
    for copy in n_z.values():
        copy.start()
    slopes(3, 0)
    word_product(3, 0)
    send_words(3)
    to_owners(1)
    region_product(1, 0, False)
    other_core(0)
    to_owners(0)

    sums = close_group(0)
    for k in (2, 1, 3):
        rx_copies[k].wait_recv()
        sums = sums + x_in[k - 1].astype(F32)
    sums = sums.reshape(NZ, OWN, D)
    halves = jnp.concatenate([sums[:, :, 0:HALF], sums[:, :, HALF:D]], axis=1)
    z_out[...] = halves.astype(BF)
    rz_copies = {
        k: send(z_out.at[(SHIFT + k) % NZ], z_in.at[k - 1], rz_send, rz_recv, k - 1, at_z(k)) for k in Z_ORDER
    }
    for k in reversed(Z_ORDER):
        rz_copies[k].start()
    chip = halves[SHIFT]
    pass_sums()

    positives = tally[1]
    for k in Z_ORDER:
        n_z[k].wait_recv()
        positives = positives + tally_z[k - 1]
    coef = (scale[0] * (1.5 / 16.0)) / positives[0:1, 0:1]

    for k in Z_ORDER:
        rz_copies[k].wait_recv()
        chip = chip + z_in[k - 1].astype(F32)
    value = jnp.concatenate([chip[0:OWN], chip[OWN:CB]], axis=1) * coef
    for cap in range(2):
        part = value[cap * TOK : (cap + 1) * TOK]
        word_out[cap] = jnp.where(TOK * z + tok < token[cap], part, 0.0).astype(BF)

    both = y_own[0]
    for k, r in ((0, 1), (1, 7), (4, 2), (5, 6)):
        ry_copies[r].wait_recv()
        both = both + y_in[k].astype(F32)
    for img in range(2):
        part = both[img * BOXP : (img + 1) * BOXP] * coef
        part = jnp.where(BOX * z + row < box[img], part, 0.0)
        region_out[img] = part[0:BOX].astype(BF)

    for copies in (z_copies, y_copies, twins, x_near, x_far, rx_copies, n_x, n_z, ry_copies, rz_copies, twin_copies):
        for copy in copies.values():
            copy.wait_send()


def on_device(
    regions,
    words,
    box_counts,
    token_counts,
    span_begin,
    span_length,
    bias_weight,
    logit_bias,
    loss_scale,
):
    vmem, in_hbm = pl.BlockSpec(memory_space=pltpu.VMEM), pl.BlockSpec(memory_space=pltpu.HBM)
    smem = pltpu.SMEM
    hold = pltpu.VMEM

    def sems(n):
        return [pltpu.SemaphoreType.DMA((n,))] * 2

    return pl.pallas_call(
        kernel,
        out_shape=(
            jax.ShapeDtypeStruct((2, BOX, D), BF),
            jax.ShapeDtypeStruct((2, TOK, D), BF),
        ),
        in_specs=[vmem] * 2 + [in_hbm] * 7,
        out_specs=(vmem, vmem),
        scratch_shapes=[
            smem((2,), jnp.int32),
            smem((2,), jnp.int32),
            smem((1,), F32),
            smem((1,), F32),
            hold((2, BOX), jnp.int32),
            hold((2, BOX), jnp.int32),
            hold((1, D), F32),
            hold((RB, D), F32),
            hold((ROWS, D), BF),
            hold((D, ROWS), BF),
            hold((8, ROWS), F32),
            hold((NX, NZ, CB, HALF), BF),
            hold((NX, GROUP, D), BF),
            hold((2, D, 2 * GP), BF),
            hold((NX, GROUP, HALF), F32),
            hold((2, 2, 2 * GP, SIDE), BF),
            hold((NX, GROUP, D), F32),
            hold((NX, GROUP, HALF), F32),
            hold((2, D, SIDE), F32),
            hold((2, PART, D), BF),
            hold((2, PART, D), BF),
            hold((NY - 1, RB, D), BF),
            hold((NY - 1, RB, D), BF),
            hold((3, RB, D), F32),
            hold((NX - 1, GROUP, D), BF),
            hold((NX - 1, GROUP, D), BF),
            hold((NZ, CB, HALF), BF),
            hold((NZ - 1, CB, HALF), BF),
            hold((2, 8, HALF), F32),
            hold((NX - 1, 8, HALF), F32),
            hold((NZ - 1, 8, HALF), F32),
            pltpu.SemaphoreType.DMA((7,)),
        ]
        + sems(NY) + sems(NZ - 1) + sems(6) + sems(NY + 2) + sems(NX + NZ - 2)
        + sems(NY) + sems(NX - 1) + sems(NZ - 1),
        compiler_params=pltpu.CompilerParams(
            collective_id=0, has_side_effects=True, vmem_limit_bytes=32 * 2**20
        ),
        name="alignment",
    )(
        regions, words, box_counts, token_counts, span_begin, span_length,
        bias_weight.reshape(1, D), logit_bias.reshape(1), loss_scale.reshape(1),
    )


def solution(mesh):
    in_specs = (
        P("dp", "text", None),
        P("dp", "text", None),
        P("dp"),
        P("dp"),
        P("dp", "text"),
        P("dp", "text"),
        P(),
        P(),
        P(),
    )
    out_specs = (P("dp", "text", None), P("dp", "text", None))
    return jax.shard_map(
        on_device, mesh=mesh, in_specs=in_specs, out_specs=out_specs, check_vma=False
    )
```
